32 devices in a mesh: seq: 8 (over z, x), head: 4 (over y, core).
Axes of the slice: x: 2, y: 2, z: 4, core: 2. Of those that a mesh axis runs over, the one named last changes fastest.
Arguments:
- token_values: bfloat16 [2048, 5120], P('seq', 'head'), may hold values from -6 to 6
- gate_values: bfloat16 [2048, 5120], P('seq', 'head'), may hold values from -30 to 30
- state_in: bfloat16 [2048, 128], P('seq'), may hold values from -0.5 to 0.5
- state_out: bfloat16 [2048, 128], P('seq'), may hold values from -6 to 6
- step_size: float32 [2048, 80], P('seq', 'head'), may hold values from 0.02 to 0.2
- log_decay: float32 [2048, 80], P('seq', 'head'), may hold values from -1 to 0
- level_weight: bfloat16 [2048, 80, 12], P('seq', 'head'), may hold values from 0.25 to 2
- skip_weight: float32 [80], P('head'), may hold values from 0.5 to 1.5
- norm_gain: float32 [5120], P('head'), may hold values from 0.1 to 1.9
- out_weight: bfloat16 [5120, 2560], P('head'), may hold values from -0.078125 to 0.078125
Outputs:
- layer_out: bfloat16 [2048, 2560], P(('seq', 'head'))
The draws below stay inside these ranges and needn't reach their ends.
All inputs are finite; a program needn't handle non-finite values.
Results may differ from the reference program's by a relative error of at most 0.014.
Values may be sent and summed in bfloat16 or wider, within the bound.
A program may use at most 64 MiB of HBM per device.

```python
import math
import jax
import jax.numpy as jnp
from jax import lax

DM = 2560
H = 80
P_SIZE = 64
N = 128
STRETCH_BITS = 6
STRETCH_DEV_BITS = 2
STRETCH = 64
TOK_DEV = 256
TOKENS = 2048
SEQ_BITS = 3
LEVELS = 12
N_HEAD = 4


def draw_log_decay(key, part):
    keys = jax.random.split(jax.random.fold_in(key, 101), 7)
    slow_share = 0.5
    slow = jax.random.uniform(keys[0], (H,)) < slow_share
    fast_rate = jnp.exp(jax.random.uniform(keys[1], (H,), minval=jnp.log(1.0 / (0.8 * STRETCH)), maxval=jnp.log(1.0 / (0.5 * STRETCH))))
    slow_rate = jnp.exp(jax.random.uniform(keys[2], (H,), minval=jnp.log(0.05), maxval=jnp.log(0.5))) / TOKENS
    fading_speed = jnp.where(slow, slow_rate, fast_rate)
    device_blocks = TOKENS // TOK_DEV
    fading_multiplier = jnp.exp(jax.random.uniform(keys[3], (device_blocks, H), minval=-0.7, maxval=0.7))
    fading_multiplier = jnp.repeat(fading_multiplier, TOK_DEV, axis=0)
    rough_guess = jnp.exp(jax.random.uniform(keys[4], (TOKENS, H), minval=jnp.log(0.5), maxval=jnp.log(1.5)))
    element_indices = jax.random.randint(keys[5], (2,), 0, TOKENS)
    blend_proportions = jax.random.uniform(keys[6], (2, H), minval=0.22, maxval=0.69)
    element_index = jnp.arange(TOKENS)[:, None]
    run_spans_count = jnp.where(element_index == element_indices[0], blend_proportions[0][None, :], 0.0) + jnp.where(element_index == element_indices[1], blend_proportions[1][None, :], 0.0)
    return jnp.clip(-(fading_speed[None, :] * fading_multiplier * rough_guess) - run_spans_count, -1.0, 0.0)


def draw_gate_values(key, part):
    keys = jax.random.split(jax.random.fold_in(key, 202), 3)
    rise = jnp.repeat(3.0 ** (jnp.arange(H, dtype=jnp.float32) / (H - 1)), P_SIZE)
    columns = rise * jnp.exp(jax.random.uniform(keys[0], (H * P_SIZE,), minval=0.0, maxval=jnp.log(3.3))) / 2.0
    scales = jnp.exp(jax.random.uniform(keys[1], (TOKENS,), minval=jnp.log(0.3), maxval=jnp.log(3.0)))
    base = jax.random.normal(keys[2], (TOKENS, H * P_SIZE))
    return jnp.clip(base * scales[:, None] * columns[None, :], -30.0, 30.0).astype(jnp.bfloat16)


def shard_levels(rng, extent, cuts, low, high):
    gain, own = 1.0, jax.random.fold_in(rng, 6)
    for axis_at, blocks in cuts:
        draws = jnp.exp(jax.random.uniform(jax.random.fold_in(own, axis_at), (blocks,), jnp.float32, low / len(cuts), high / len(cuts)))
        gain = gain * jnp.repeat(draws, extent[axis_at] // blocks).reshape([-1 if axis == axis_at else 1 for axis in range(len(extent))])
    return gain


def bell_draw(stream_key, extent, spread, reach, shards=(), kind=jnp.bfloat16):
    values = spread * jax.random.normal(stream_key, extent, jnp.float32)
    if shards:
        values = values * shard_levels(stream_key, extent, shards, -0.22, 0.18)
    return jnp.clip(values, -reach, reach).astype(kind)


def setup_inputs(seed: int = 0) -> dict:
    arg_keys = jax.random.split(jax.random.key(seed), 11)
    token_values = bell_draw(arg_keys[0], (TOKENS, H * P_SIZE), 1.0, 6.0, ((0, 8), (1, 4)))
    gate_values = draw_gate_values(jax.random.fold_in(arg_keys[10], 71), 0)
    state_in = bell_draw(arg_keys[2], (TOKENS, N), N ** -0.5, 0.5, ((0, 8),))
    state_out = bell_draw(arg_keys[3], (TOKENS, N), 1.0, 6.0, ((0, 8),))
    step_size = jnp.clip(jnp.exp(math.log(0.2) - 2.3025851 * jax.random.uniform(arg_keys[4], (TOKENS, H), jnp.float32) ** shard_levels(arg_keys[4], (TOKENS, H), ((0, 8), (1, 4)), -0.2, 0.2)), 0.02, 0.2)
    log_decay = draw_log_decay(jax.random.fold_in(arg_keys[10], 71), 0)
    level_weight = jnp.clip(jnp.exp(math.log(2.0) - 2.0794415 * jax.random.uniform(arg_keys[6], (TOKENS, H, LEVELS), jnp.float32) ** shard_levels(arg_keys[6], (TOKENS, H, LEVELS), ((0, 8), (1, 4)), -0.2, 0.2)), 0.25, 2.0).astype(jnp.bfloat16)
    skip_weight = jnp.clip(0.5 + 1.0 * jax.random.uniform(arg_keys[7], (H,), jnp.float32) ** shard_levels(arg_keys[7], (H,), ((0, 4),), -0.2, 0.2), 0.5, 1.5)
    norm_gain = jnp.clip(1.0 + 0.18 * jax.random.normal(arg_keys[8], (H * P_SIZE,), jnp.float32), 0.1, 1.9)
    out_weight = bell_draw(arg_keys[9], (H * P_SIZE, DM), (H * P_SIZE) ** -0.5, 0.078125, ((0, 4),))
    return {"token_values": token_values, "gate_values": gate_values, "state_in": state_in, "state_out": state_out, "step_size": step_size, "log_decay": log_decay, "level_weight": level_weight, "skip_weight": skip_weight, "norm_gain": norm_gain, "out_weight": out_weight}


EPSILON = 1e-05
HIGH = lax.Precision.HIGHEST

def bit_count(values, bit_width):
    counted = jnp.zeros(values.shape, jnp.int32)
    for shift in range(bit_width):
        counted = counted + (values >= 1 << shift).astype(jnp.int32)
    return counted

def stretch_levels():
    inside = jnp.arange(STRETCH, dtype=jnp.int32)
    later = inside[:, None]
    earlier = inside[None, :]
    causal = earlier <= later
    levels = bit_count(jnp.bitwise_xor(later, earlier), STRETCH_BITS)
    onehot = (levels[:, :, None] == jnp.arange(STRETCH_BITS + 1, dtype=jnp.int32)[None, None, :]) & causal[:, :, None]
    return (causal, onehot.astype(jnp.float32))

def head_mix(scores, query_rows, key_rows, causal, onehot, packed):
    values, steps, decays, weights, skip = packed
    blocks_all = TOKENS // STRETCH
    inputs = (values * steps[:, None]).reshape(blocks_all, STRETCH, P_SIZE)
    within = jnp.cumsum(decays.reshape(blocks_all, STRETCH), axis=1)
    totals = within[:, -1]
    weights = weights.reshape(blocks_all, STRETCH, LEVELS)
    gaps = jnp.where(causal[None], within[:, :, None] - within[:, None, :], -jnp.inf)
    mixing = jnp.einsum('ctl,tsl->cts', weights[:, :, :STRETCH_BITS + 1], onehot) * jnp.exp(gaps) * scores
    output = jnp.einsum('cts,csp->ctp', mixing, inputs, precision=HIGH)
    to_end = jnp.exp(totals[:, None] - within)
    states = jnp.einsum('csn,csp->cnp', key_rows * to_end[:, :, None], inputs, precision=HIGH)
    queries = query_rows * jnp.exp(within)[:, :, None]
    block_ids = jnp.arange(blocks_all, dtype=jnp.int32)
    blocks = states
    block_totals = totals
    for depth in range(1, STRETCH_DEV_BITS + SEQ_BITS + 1):
        size = 2 ** (depth - 1)
        grouped = totals.reshape(blocks_all // size, size)
        before = (jnp.cumsum(grouped, axis=1) - grouped).reshape(blocks_all)
        upper = (block_ids >> depth - 1 & 1).astype(jnp.float32)
        sibling = jnp.bitwise_xor(block_ids >> depth - 1, 1).astype(jnp.int32)
        carried = blocks[sibling] * (upper * jnp.exp(before))[:, None, None]
        reached = jnp.einsum('ctn,cnp->ctp', queries, carried, precision=HIGH)
        output = output + weights[:, :, STRETCH_BITS + depth, None] * reached
        paired = blocks.reshape(-1, 2, N, P_SIZE)
        pair_totals = block_totals.reshape(-1, 2)
        blocks = jnp.exp(pair_totals[:, 1])[:, None, None] * paired[:, 0] + paired[:, 1]
        block_totals = pair_totals[:, 0] + pair_totals[:, 1]
    return output.reshape(TOKENS, P_SIZE) + skip * values

def reference(token_values, gate_values, state_in, state_out, step_size, log_decay, level_weight, skip_weight, norm_gain, out_weight):
    blocks_all = TOKENS // STRETCH
    causal, onehot = stretch_levels()
    query_rows = state_out.astype(jnp.float32).reshape(blocks_all, STRETCH, N)
    key_rows = state_in.astype(jnp.float32).reshape(blocks_all, STRETCH, N)
    scores = jnp.einsum('ctn,csn->cts', query_rows, key_rows)
    values_heads = jnp.transpose(token_values.astype(jnp.float32).reshape(TOKENS, H, P_SIZE), (1, 0, 2))
    steps_heads = jnp.transpose(step_size)
    decays_heads = jnp.transpose(log_decay)
    weights_heads = jnp.transpose(level_weight.astype(jnp.float32), (1, 0, 2))

    def per_head(packed):
        return head_mix(scores, query_rows, key_rows, causal, onehot, packed)
    mixed_heads = lax.map(per_head, (values_heads, steps_heads, decays_heads, weights_heads, skip_weight))
    mixed = jnp.transpose(mixed_heads, (1, 0, 2)).reshape(TOKENS, H * P_SIZE)
    gated = mixed * jax.nn.silu(gate_values.astype(jnp.float32))
    square = lax.optimization_barrier(jnp.mean(gated * gated, axis=1, keepdims=True))
    features = (gated * lax.rsqrt(square + EPSILON) * norm_gain).astype(jnp.bfloat16)
    width = H * P_SIZE // N_HEAD

    def add_group(total, group):
        picked = lax.dynamic_slice_in_dim(features, group * width, width, 1)
        rows_w = lax.dynamic_slice_in_dim(out_weight, group * width, width, 0)
        partial_value = jnp.dot(picked, rows_w, preferred_element_type=jnp.float32).astype(jnp.bfloat16)
        return (total + partial_value.astype(jnp.float32), None)
    summed, _ = lax.scan(add_group, jnp.zeros((TOKENS, DM), jnp.float32), jnp.arange(N_HEAD, dtype=jnp.int32))
    return summed.astype(jnp.bfloat16)
```

```python
import functools

import jax
import jax.numpy as jnp
from jax import lax
from jax.experimental import pallas as pl
from jax.experimental.pallas import tpu as pltpu
from jax.sharding import PartitionSpec as P

P_SIZE = 64
EPSILON = 1e-05
HIGH = lax.Precision.HIGHEST
MESH = pl.DeviceIdType.MESH
LANES = 128
F32 = jnp.float32
BF16 = jnp.bfloat16


def dot(a, b, precision=None):
    return jnp.dot(a, b, preferred_element_type=F32, precision=precision)


def dot_nt(a, b):
    return lax.dot_general(a, b, (((1,), (1,)), ((), ())), preferred_element_type=F32)


def partner_of(axis, depth):
    me = lax.axis_index(axis)
    bit = (me // 2**depth) % 2
    return bit, me + (1 - 2 * bit) * 2**depth


def mixer_kernel(
    seq_bits,
    width_all,
    col,
    GROUP,
    head_devices,
    tv_ref,
    gate_ref,
    key_ref,
    query_ref,
    step_ref,
    decay_ref,
    weight_ref,
    skip_ref,
    gain_ref,
    w_hbm,
    out_ref,
    w_ref,
    tvt,
    xt,
    mixed,
    silu_t,
    gain_t,
    feat,
    lw,
    cum_r,
    cum_c,
    lift,
    score_t,
    level_of,
    own,
    got,
    e_own,
    e_got,
    factor,
    square,
    sq_send,
    sq_got,
    core_send,
    core_got,
    far_send,
    far_got,
    w_sem,
    state_ss,
    state_rs,
    e_ss,
    e_rs,
    sq_ss,
    sq_rs,
    core_ss,
    core_rs,
    far_ss,
    far_rs,
):
    rows = tv_ref.shape[0]
    heads = step_ref.shape[0]
    tiles = rows // LANES
    groups = heads // GROUP
    span = GROUP * P_SIZE
    lane_bits = LANES.bit_length() - 1
    local_bits = rows.bit_length() - 1
    levels_here = local_bits + 1
    n_col = w_ref.shape[1] // col
    block = rows // head_devices
    chips = head_devices // 2

    barrier = pltpu.get_barrier_semaphore()
    seq_partner = [partner_of("seq", d) for d in range(seq_bits)]
    core_bit, core_peer = partner_of("head", 0)
    chip = lax.axis_index("head") // 2
    chip_at = [(chip + r) % chips for r in range(chips)]
    far_peer = [2 * at + core_bit for at in chip_at]
    for _, peer in seq_partner:
        pl.semaphore_signal(barrier, inc=1, device_id={"seq": peer}, device_id_type=MESH)
    for peer in [core_peer] + far_peer[1:]:
        pl.semaphore_signal(barrier, inc=1, device_id={"head": peer}, device_id_type=MESH)

    w_copy = pltpu.make_async_copy(w_hbm, w_ref, w_sem)
    w_copy.start()

    def send(axis, peer, src, dst, ss, rs):
        return pltpu.make_async_remote_copy(
            src_ref=src,
            dst_ref=dst,
            send_sem=ss,
            recv_sem=rs,
            device_id={axis: peer},
            device_id_type=MESH,
        )

    def state_copy(d, g):
        return send(
            "seq", seq_partner[d][1], own.at[d, g], got.at[d, g], state_ss.at[d, g], state_rs.at[d, g]
        )

    def total_copy(d):
        return send("seq", seq_partner[d][1], e_own.at[d], e_got.at[d], e_ss.at[d], e_rs.at[d])

    u_at = lax.broadcasted_iota(jnp.int32, (rows, rows), 0)
    t_at = lax.broadcasted_iota(jnp.int32, (rows, rows), 1)
    decay = decay_ref[...]
    cum = dot(decay, (u_at <= t_at).astype(F32), HIGH)
    to_end = jnp.exp(dot(decay, (u_at > t_at).astype(F32), HIGH))
    total = dot(decay, jnp.ones((rows, LANES), F32), HIGH)
    cum_r[...] = cum
    steps = step_ref[...]
    key_scale = steps * to_end
    e_own[0] = jnp.exp(total)

    for j in range(tv_ref.shape[1] // LANES):
        tvt[pl.ds(j * LANES, LANES), :] = jnp.transpose(
            tv_ref[:, pl.ds(j * LANES, LANES)].astype(F32)
        )

    pl.semaphore_wait(barrier, seq_bits + chips)
    total_copy(0).start()
    keys = key_ref[...]
    for g in range(groups):
        parts = []
        for h in range(g * GROUP, (g + 1) * GROUP):
            value = tvt[pl.ds(h * P_SIZE, P_SIZE), :]
            parts.append((value * key_scale[h : h + 1, :]).astype(BF16))
            xt[pl.ds(h * P_SIZE, P_SIZE), :] = (value * steps[h : h + 1, :]).astype(BF16)
        own[0, g] = dot(jnp.concatenate(parts, axis=0), keys).astype(BF16)
        state_copy(0, g).start()

    lift[...] = jnp.exp(cum)
    cum_c[...] = jnp.transpose(cum)
    for l in range(weight_ref.shape[0]):
        lw[l] = weight_ref[l].astype(F32)
    queries = query_ref[...]
    s_full = dot_nt(keys, queries)
    score_t[...] = jnp.where(u_at <= t_at, s_full, 0.0)
    apart = jnp.bitwise_xor(u_at[:LANES, :LANES], t_at[:LANES, :LANES])
    level = jnp.zeros((LANES, LANES), jnp.int32)
    for shift in range(lane_bits):
        level = level + (apart >= 1 << shift).astype(jnp.int32)
    level_of[...] = level
    square[...] = jnp.zeros_like(square)
    for j in range(gate_ref.shape[1] // LANES):
        gain_t[pl.ds(j * LANES, LANES), :] = jnp.transpose(
            jnp.broadcast_to(gain_ref[:, pl.ds(j * LANES, LANES)], (LANES, LANES))
        )

    def local_part(g):
        for h in range(g * GROUP, (g + 1) * GROUP):
            at = pl.ds(h * P_SIZE, P_SIZE)
            x = xt[at, :]
            for bt in range(tiles):
                lanes = pl.ds(bt * LANES, LANES)
                row = cum_r[pl.ds(h, 1), lanes]
                stack = []
                for bs in range(bt + 1):
                    sub = pl.ds(bs * LANES, LANES)
                    column = cum_c[sub, pl.ds(h, 1)]
                    fade = jnp.exp(jnp.minimum(row - column, 0.0)) * score_t[sub, lanes]
                    if bs == bt:
                        level_now = level_of[...]
                        weight = jnp.broadcast_to(lw[0, pl.ds(h, 1), lanes], (LANES, LANES))
                        for l in range(1, lane_bits + 1):
                            weight = jnp.where(level_now == l, lw[l, pl.ds(h, 1), lanes], weight)
                    else:
                        weight = lw[lane_bits + (bt ^ bs).bit_length(), pl.ds(h, 1), lanes]
                    stack.append((fade * weight).astype(BF16))
                mix = stack[0] if bt == 0 else jnp.concatenate(stack, axis=0)
                mixed[at, lanes] = dot(x[:, : (bt + 1) * LANES], mix) + skip_ref[h] * tvt[at, lanes]
        for j in range(g * span // LANES, (g + 1) * span // LANES):
            gate = jnp.transpose(gate_ref[:, pl.ds(j * LANES, LANES)].astype(F32))
            silu_t[pl.ds(j * LANES, LANES), :] = gate / (1.0 + jnp.exp(-gate))

    def far_part(d, g):
        bit, _ = seq_partner[d]
        up = bit.astype(F32)
        if g == 0:
            total_copy(d).wait()
            mine, theirs = e_own[d], e_got[d]
            reach = jnp.ones_like(mine) if d == 0 else factor[d]
            if d + 1 < seq_bits:
                factor[d + 1] = reach * (up * theirs + (1.0 - up))
                e_own[d + 1] = mine * theirs
                total_copy(d + 1).start()
        state_copy(d, g).wait_recv()
        if d + 1 < seq_bits:
            mine, theirs = e_own[d], e_got[d]
            keep = up + (1.0 - up) * theirs
            take = up * mine + (1.0 - up)
            for i in range(GROUP):
                h = g * GROUP + i
                at = pl.ds(i * P_SIZE, P_SIZE)
                own[d + 1, g, at, :] = (
                    own[d, g, at, :].astype(F32) * keep[h : h + 1, :]
                    + got[d, g, at, :].astype(F32) * take[h : h + 1, :]
                ).astype(BF16)
            state_copy(d + 1, g).start()
        reached = dot_nt(got[d, g], query_ref[...])
        for i in range(GROUP):
            h = g * GROUP + i
            at = pl.ds(h * P_SIZE, P_SIZE)
            scale = lw[levels_here + d, pl.ds(h, 1), :] * lift[pl.ds(h, 1), :] * up
            if d > 0:
                reach = factor[d, pl.ds(h, 1), :]
                scale = scale * jnp.concatenate([reach] * tiles, axis=1)
            mixed[at, :] += reached[i * P_SIZE : (i + 1) * P_SIZE] * scale

    def finish_group(g):
        at = pl.ds(g * span, span)
        gated = mixed[at, :] * silu_t[at, :]
        square[...] += jnp.sum((gated * gated).reshape(span // 8, 8, rows), axis=0)
        gain = jnp.concatenate([gain_t[at, :]] * tiles, axis=1)
        feat[:, at] = jnp.transpose(gated * gain).astype(BF16)

    for k in range(groups + seq_bits):
        if k < groups:
            local_part(k)
        for d in range(seq_bits):
            g = k - d
            if 0 <= g < groups:
                far_part(d, g)
                if d == seq_bits - 1:
                    finish_group(g)

    sq_send[0] = square[...]
    sq_core = send("head", core_peer, sq_send.at[0], sq_got.at[0], sq_ss.at[0], sq_rs.at[0])
    sq_core.start()
    w_copy.wait()

    def core_copy(part, j):
        return send(
            "head",
            core_peer,
            core_send.at[part, j],
            core_got.at[part, j],
            core_ss.at[part, j],
            core_rs.at[part, j],
        )

    def far_copy(r, j):
        return send(
            "head",
            far_peer[r],
            far_send.at[r - 1, j],
            far_got.at[r - 1, j],
            far_ss.at[r - 1, j],
            far_rs.at[r - 1, j],
        )

    mine_at = core_bit * block
    theirs_at = (1 - core_bit) * block

    def project(r, j):
        wide = pl.ds(j * col, col)
        at = chip_at[r] * (2 * block)
        theirs = feat[pl.ds(pl.multiple_of(at + theirs_at, block), block), :]
        mine = feat[pl.ds(pl.multiple_of(at + mine_at, block), block), :]
        product = dot(jnp.concatenate([theirs, mine], axis=0), w_ref[:, wide])
        core_send[r, j] = product[:block].astype(BF16)
        core_copy(r, j).start()
        return product[block:]

    def forward(r, j, value):
        core_copy(r, j).wait_recv()
        far_send[r - 1, j] = (value + core_got[r, j].astype(F32)).astype(BF16)
        far_copy(r, j).start()

    held = None
    for r in range(1, chips):
        for j in range(n_col):
            fresh = project(r, j)
            if held is not None:
                forward(*held)
            held = (r, j, fresh)
    sq_core.wait()
    pair_square = square[...] + sq_got[0]
    sq_send[1] = pair_square
    sq_far = [
        send(
            "head", far_peer[r], sq_send.at[1], sq_got.at[r], sq_ss.at[r], sq_rs.at[r]
        )
        for r in range(1, chips)
    ]
    for copy in sq_far:
        copy.start()
    kept = []
    for j in range(n_col):
        kept.append(project(0, j))
        if j == 0:
            forward(*held)
    for copy in sq_far:
        copy.wait()
    for r in range(1, chips):
        pair_square = pair_square + sq_got[r]
    total_square = jnp.sum(pair_square, axis=0, keepdims=True)
    norm = lax.rsqrt(total_square / width_all + EPSILON)
    columns = jnp.transpose(jnp.broadcast_to(norm, (LANES, rows)))
    gain_t[pl.ds(0, rows), :] = columns
    me = lax.axis_index("head")
    norm_mine = gain_t[pl.ds(pl.multiple_of(me * block, block), block), :]
    norm_wide = jnp.concatenate([norm_mine] * (col // LANES), axis=1)
    for j in range(n_col):
        core_copy(0, j).wait_recv()
        value = kept[j] + core_got[0, j].astype(F32)
        for r in range(1, chips):
            far_copy(r, j).wait_recv()
            value = value + far_got[r - 1, j].astype(F32)
        out_ref[:, pl.ds(j * col, col)] = (value * norm_wide).astype(BF16)

    for j in range(n_col):
        for r in range(chips):
            core_copy(r, j).wait_send()
        for r in range(1, chips):
            far_copy(r, j).wait_send()
    for d in range(seq_bits):
        for g in range(groups):
            state_copy(d, g).wait_send()


def on_device(
    token_values,
    gate_values,
    state_in,
    state_out,
    step_size,
    log_decay,
    level_weight,
    skip_weight,
    norm_gain,
    out_weight,
):
    rows, width = token_values.shape
    heads = step_size.shape[1]
    n_state = state_in.shape[1]
    levels = level_weight.shape[2]
    model = out_weight.shape[1]
    seq_bits = lax.axis_size("seq").bit_length() - 1
    head_devices = lax.axis_size("head")
    group = 4 if heads % 4 == 0 else 2
    groups = heads // group
    span = group * P_SIZE
    chips = head_devices // 2
    col = 512
    n_col = model // col
    block = rows // head_devices
    vmem = pl.BlockSpec(memory_space=pltpu.VMEM)
    dma = pltpu.SemaphoreType.DMA
    scratch = [
        pltpu.VMEM((width, model), BF16),
        pltpu.VMEM((width, rows), F32),
        pltpu.VMEM((width, rows), BF16),
        pltpu.VMEM((width, rows), F32),
        pltpu.VMEM((width, rows), F32),
        pltpu.VMEM((width, LANES), F32),
        pltpu.VMEM((rows, width), BF16),
        pltpu.VMEM((levels, heads, rows), F32),
        pltpu.VMEM((heads, rows), F32),
        pltpu.VMEM((rows, heads), F32),
        pltpu.VMEM((heads, rows), F32),
        pltpu.VMEM((rows, rows), F32),
        pltpu.VMEM((LANES, LANES), jnp.int32),
        pltpu.VMEM((seq_bits, groups, span, n_state), BF16),
        pltpu.VMEM((seq_bits, groups, span, n_state), BF16),
        pltpu.VMEM((seq_bits, heads, LANES), F32),
        pltpu.VMEM((seq_bits, heads, LANES), F32),
        pltpu.VMEM((seq_bits, heads, LANES), F32),
        pltpu.VMEM((8, rows), F32),
        pltpu.VMEM((2, 8, rows), F32),
        pltpu.VMEM((chips, 8, rows), F32),
        pltpu.VMEM((chips, n_col, block, col), BF16),
        pltpu.VMEM((chips, n_col, block, col), BF16),
        pltpu.VMEM((chips - 1, n_col, block, col), BF16),
        pltpu.VMEM((chips - 1, n_col, block, col), BF16),
        dma,
        dma((seq_bits, groups)),
        dma((seq_bits, groups)),
        dma((seq_bits,)),
        dma((seq_bits,)),
        dma((chips,)),
        dma((chips,)),
        dma((chips, n_col)),
        dma((chips, n_col)),
        dma((chips - 1, n_col)),
        dma((chips - 1, n_col)),
    ]
    return pl.pallas_call(
        functools.partial(
            mixer_kernel, seq_bits, float(width * head_devices), col, group, head_devices
        ),
        out_shape=jax.ShapeDtypeStruct((block, model), BF16),
        in_specs=[vmem] * 7
        + [pl.BlockSpec(memory_space=pltpu.SMEM), vmem, pl.BlockSpec(memory_space=pl.ANY)],
        out_specs=vmem,
        scratch_shapes=scratch,
        compiler_params=pltpu.CompilerParams(
            collective_id=0, has_side_effects=True, vmem_limit_bytes=48 * 1024 * 1024
        ),
        cost_estimate=pl.CostEstimate(
            flops=2 * rows * width * (model + 4 * rows), bytes_accessed=2 * width * model, transcendentals=heads * rows * rows
        ),
        name="mixer",
    )(
        token_values,
        gate_values,
        state_in,
        state_out,
        jnp.transpose(step_size),
        jnp.transpose(log_decay),
        jnp.transpose(level_weight, (2, 1, 0)),
        skip_weight,
        norm_gain.reshape(1, width),
        out_weight,
    )


def solution(mesh):
    placed = (
        P("seq", "head"),
        P("seq", "head"),
        P("seq", None),
        P("seq", None),
        P("seq", "head"),
        P("seq", "head"),
        P("seq", "head", None),
        P("head"),
        P("head"),
        P("head", None),
    )
    return jax.shard_map(
        on_device, mesh=mesh, in_specs=placed, out_specs=P(("seq", "head"), None), check_vma=False
    )
```

```python
import functools

import jax
import jax.numpy as jnp
from jax import lax
from jax.experimental import pallas as pl
from jax.experimental.pallas import tpu as pltpu
from jax.sharding import PartitionSpec as P

P_SIZE = 64
EPSILON = 1e-05
HIGH = lax.Precision.HIGHEST
MESH = pl.DeviceIdType.MESH
LANES = 128
F32 = jnp.float32
BF16 = jnp.bfloat16


def dot(a, b, precision=None):
    return jnp.dot(a, b, preferred_element_type=F32, precision=precision)


def dot_nt(a, b):
    return lax.dot_general(a, b, (((1,), (1,)), ((), ())), preferred_element_type=F32)


def partner_of(axis, depth):
    me = lax.axis_index(axis)
    bit = (me // 2**depth) % 2
    return bit, me + (1 - 2 * bit) * 2**depth


def mixer_kernel(
    seq_bits,
    width_all,
    col,
    GROUP,
    head_devices,
    tv_hbm,
    gate_hbm,
    key_hbm,
    query_hbm,
    step_hbm,
    decay_hbm,
    weight_hbm,
    skip_ref,
    gain_hbm,
    w_hbm,
    out_ref,
    tv_ref,
    gate_ref,
    key_ref,
    query_ref,
    step_ref,
    decay_ref,
    weight_ref,
    gain_ref,
    w_ref,
    tvt,
    xt,
    mixed,
    silu_t,
    gain_t,
    feat,
    lw,
    cum_r,
    cum_c,
    lift,
    score_t,
    level_of,
    own,
    got,
    e_own,
    e_got,
    factor,
    square,
    sq_send,
    sq_got,
    core_send,
    core_got,
    far_send,
    far_got,
    w_sem,
    state_ss,
    state_rs,
    e_ss,
    e_rs,
    sq_ss,
    sq_rs,
    core_ss,
    core_rs,
    far_ss,
    far_rs,
    in_sem,
    side_ss,
):
    rows = tv_ref.shape[0]
    heads = step_ref.shape[0]
    tiles = rows // LANES
    groups = heads // GROUP
    span = GROUP * P_SIZE
    lane_bits = LANES.bit_length() - 1
    local_bits = rows.bit_length() - 1
    levels_here = local_bits + 1
    n_col = w_ref.shape[1] // col
    block = rows // head_devices
    chips = head_devices // 2

    barrier = pltpu.get_barrier_semaphore()
    seq_partner = [partner_of("seq", d) for d in range(seq_bits)]
    core_bit, core_peer = partner_of("head", 0)
    chip = lax.axis_index("head") // 2
    chip_at = [(chip + r) % chips for r in range(chips)]
    far_peer = [2 * at + core_bit for at in chip_at]
    last = seq_bits - 1
    n_seq = 2**seq_bits
    stride = 2 ** (seq_bits // 2)
    at_seq = lax.axis_index("seq")
    onward = (at_seq + stride) % n_seq
    behind = (at_seq + n_seq - stride) % n_seq
    is_up = at_seq >= n_seq // 2
    has_next = at_seq + stride < n_seq
    is_source = jnp.logical_and(at_seq < n_seq // 2, at_seq + stride >= n_seq // 2)
    for peer in [p for _, p in seq_partner[:last]] + [onward, behind]:
        pl.semaphore_signal(barrier, inc=1, device_id={"seq": peer}, device_id_type=MESH)
    for peer in [core_peer] + far_peer[1:]:
        pl.semaphore_signal(barrier, inc=1, device_id={"head": peer}, device_id_type=MESH)

    pairs = [
        (decay_hbm, decay_ref),
        (step_hbm, step_ref),
        (tv_hbm, tv_ref),
        (key_hbm, key_ref),
        (query_hbm, query_ref),
        (weight_hbm, weight_ref),
        (gate_hbm, gate_ref),
        (gain_hbm, gain_ref),
    ]
    loads = [
        pltpu.make_async_copy(src, dst, in_sem.at[i]) for i, (src, dst) in enumerate(pairs)
    ]
    w_copy = pltpu.make_async_copy(w_hbm, w_ref, w_sem)
    for load in loads:
        load.start()
    w_copy.start()

    def send(axis, peer, src, dst, ss, rs):
        return pltpu.make_async_remote_copy(
            src_ref=src,
            dst_ref=dst,
            send_sem=ss,
            recv_sem=rs,
            device_id={axis: peer},
            device_id_type=MESH,
        )

    def state_copy(d, g):
        return send(
            "seq", seq_partner[d][1], own.at[d, g], got.at[d, g], state_ss.at[d, g], state_rs.at[d, g]
        )

    def total_copy(d):
        return send("seq", seq_partner[d][1], e_own.at[d], e_got.at[d], e_ss.at[d], e_rs.at[d])

    def turn(g):
        return at_seq % 2 == g % 2

    def cross_copy(g):
        return send(
            "seq", onward, own.at[last, g], got.at[last, g], state_ss.at[last, g], state_rs.at[last, g]
        )

    def onward_copy(g):
        return send(
            "seq", onward, got.at[last, g], got.at[last, g], state_ss.at[last, g], state_rs.at[last, g]
        )

    def side_copy(g):
        return send(
            "seq",
            seq_partner[0][1],
            got.at[last, g],
            got.at[last, g],
            side_ss.at[g],
            state_rs.at[last, g],
        )

    u_at = lax.broadcasted_iota(jnp.int32, (rows, rows), 0)
    t_at = lax.broadcasted_iota(jnp.int32, (rows, rows), 1)
    loads[0].wait()
    decay = decay_ref[...]
    cum = dot(decay, (u_at <= t_at).astype(F32), HIGH)
    to_end = jnp.exp(dot(decay, (u_at > t_at).astype(F32), HIGH))
    total = dot(decay, jnp.ones((rows, LANES), F32), HIGH)
    cum_r[...] = cum
    loads[1].wait()
    steps = step_ref[...]
    key_scale = steps * to_end
    e_own[0] = jnp.exp(total)

    loads[2].wait()
    loads[3].wait()
    pl.semaphore_wait(barrier, last + 2 + chips)
    total_copy(0).start()
    keys = key_ref[...]
    for g in range(groups):
        for j in range(g * span // LANES, (g + 1) * span // LANES):
            tvt[pl.ds(j * LANES, LANES), :] = jnp.transpose(
                tv_ref[:, pl.ds(j * LANES, LANES)].astype(F32)
            )
        parts = []
        for h in range(g * GROUP, (g + 1) * GROUP):
            value = tvt[pl.ds(h * P_SIZE, P_SIZE), :]
            parts.append((value * key_scale[h : h + 1, :]).astype(BF16))
            xt[pl.ds(h * P_SIZE, P_SIZE), :] = (value * steps[h : h + 1, :]).astype(BF16)
        own[0, g] = dot(jnp.concatenate(parts, axis=0), keys).astype(BF16)
        state_copy(0, g).start()

    for load in loads[4:]:
        load.wait()
    lift[...] = jnp.exp(cum)
    cum_c[...] = jnp.transpose(cum)
    for l in range(weight_ref.shape[0]):
        lw[l] = weight_ref[l].astype(F32)
    queries = query_ref[...]
    s_full = dot_nt(keys, queries)
    score_t[...] = jnp.where(u_at <= t_at, s_full, 0.0)
    apart = jnp.bitwise_xor(u_at[:LANES, :LANES], t_at[:LANES, :LANES])
    level = jnp.zeros((LANES, LANES), jnp.int32)
    for shift in range(lane_bits):
        level = level + (apart >= 1 << shift).astype(jnp.int32)
    level_of[...] = level
    square[...] = jnp.zeros_like(square)
    for j in range(gate_ref.shape[1] // LANES):
        gain_t[pl.ds(j * LANES, LANES), :] = jnp.transpose(
            jnp.broadcast_to(gain_ref[pl.ds(j * LANES, LANES)].reshape(1, LANES), (LANES, LANES))
        )

    def local_part(g):
        for h in range(g * GROUP, (g + 1) * GROUP):
            at = pl.ds(h * P_SIZE, P_SIZE)
            x = xt[at, :]
            for bt in range(tiles):
                lanes = pl.ds(bt * LANES, LANES)
                row = cum_r[pl.ds(h, 1), lanes]
                stack = []
                for bs in range(bt + 1):
                    sub = pl.ds(bs * LANES, LANES)
                    column = cum_c[sub, pl.ds(h, 1)]
                    fade = jnp.exp(jnp.minimum(row - column, 0.0)) * score_t[sub, lanes]
                    if bs == bt:
                        level_now = level_of[...]
                        weight = jnp.broadcast_to(lw[0, pl.ds(h, 1), lanes], (LANES, LANES))
                        for l in range(1, lane_bits + 1):
                            weight = jnp.where(level_now == l, lw[l, pl.ds(h, 1), lanes], weight)
                    else:
                        weight = lw[lane_bits + (bt ^ bs).bit_length(), pl.ds(h, 1), lanes]
                    stack.append((fade * weight).astype(BF16))
                mix = stack[0] if bt == 0 else jnp.concatenate(stack, axis=0)
                mixed[at, lanes] = dot(x[:, : (bt + 1) * LANES], mix) + skip_ref[h] * tvt[at, lanes]
        for j in range(g * span // LANES, (g + 1) * span // LANES):
            gate = jnp.transpose(gate_ref[:, pl.ds(j * LANES, LANES)].astype(F32))
            silu_t[pl.ds(j * LANES, LANES), :] = gate / (1.0 + jnp.exp(-gate))

    def add_far(d, g, up):
        reached = dot_nt(got[d, g], query_ref[...])
        for i in range(GROUP):
            h = g * GROUP + i
            at = pl.ds(h * P_SIZE, P_SIZE)
            scale = lw[levels_here + d, pl.ds(h, 1), :] * lift[pl.ds(h, 1), :] * up
            if d > 0:
                reach = factor[d, pl.ds(h, 1), :]
                scale = scale * jnp.concatenate([reach] * tiles, axis=1)
            mixed[at, :] += reached[i * P_SIZE : (i + 1) * P_SIZE] * scale

    def far_part(d, g):
        bit, _ = seq_partner[d]
        up = bit.astype(F32)
        if g == 0:
            total_copy(d).wait()
            mine, theirs = e_own[d], e_got[d]
            reach = jnp.ones_like(mine) if d == 0 else factor[d]
            factor[d + 1] = reach * (up * theirs + (1.0 - up))
            if d + 1 < last:
                e_own[d + 1] = mine * theirs
                total_copy(d + 1).start()
        state_copy(d, g).wait_recv()
        mine, theirs = e_own[d], e_got[d]
        keep = up + (1.0 - up) * theirs
        take = up * mine + (1.0 - up)
        for i in range(GROUP):
            h = g * GROUP + i
            at = pl.ds(i * P_SIZE, P_SIZE)
            own[d + 1, g, at, :] = (
                own[d, g, at, :].astype(F32) * keep[h : h + 1, :]
                + got[d, g, at, :].astype(F32) * take[h : h + 1, :]
            ).astype(BF16)
        if d + 1 < last:
            state_copy(d + 1, g).start()
        else:

            @pl.when(jnp.logical_and(is_source, turn(g)))
            def _():
                cross_copy(g).start()

        add_far(d, g, up)

    def last_part(g):
        @pl.when(is_up)
        def _():
            side_copy(g).wait_recv()

            @pl.when(turn(g))
            def _():
                side_copy(g).start()

            @pl.when(jnp.logical_and(turn(g), has_next))
            def _():
                onward_copy(g).start()

            add_far(last, g, 1.0)

    def finish_group(g):
        at = pl.ds(g * span, span)
        gated = mixed[at, :] * silu_t[at, :]
        square[...] += jnp.sum((gated * gated).reshape(span // 8, 8, rows), axis=0)
        gain = jnp.concatenate([gain_t[at, :]] * tiles, axis=1)
        feat[:, at] = jnp.transpose(gated * gain).astype(BF16)

    for k in range(groups + seq_bits):
        if k < groups:
            local_part(k)
        for d in range(seq_bits):
            g = k - d
            if 0 <= g < groups:
                if d < last:
                    far_part(d, g)
                else:
                    last_part(g)
                    finish_group(g)

    sq_send[0] = square[...]
    sq_core = send("head", core_peer, sq_send.at[0], sq_got.at[0], sq_ss.at[0], sq_rs.at[0])
    sq_core.start()
    w_copy.wait()

    def core_copy(part, j):
        return send(
            "head",
            core_peer,
            core_send.at[part, j],
            core_got.at[part, j],
            core_ss.at[part, j],
            core_rs.at[part, j],
        )

    def far_copy(r, j):
        return send(
            "head",
            far_peer[r],
            far_send.at[r - 1, j],
            far_got.at[r - 1, j],
            far_ss.at[r - 1, j],
            far_rs.at[r - 1, j],
        )

    mine_at = core_bit * block
    theirs_at = (1 - core_bit) * block

    def project(r, j):
        wide = pl.ds(j * col, col)
        at = chip_at[r] * (2 * block)
        theirs = feat[pl.ds(pl.multiple_of(at + theirs_at, block), block), :]
        mine = feat[pl.ds(pl.multiple_of(at + mine_at, block), block), :]
        product = dot(jnp.concatenate([theirs, mine], axis=0), w_ref[:, wide])
        core_send[r, j] = product[:block].astype(BF16)
        core_copy(r, j).start()
        return product[block:]

    def forward(r, j, value):
        core_copy(r, j).wait_recv()
        far_send[r - 1, j] = (value + core_got[r, j].astype(F32)).astype(BF16)
        far_copy(r, j).start()

    held = None
    for r in range(1, chips):
        for j in range(n_col):
            fresh = project(r, j)
            if held is not None:
                forward(*held)
            held = (r, j, fresh)
    sq_core.wait()
    pair_square = square[...] + sq_got[0]
    sq_send[1] = pair_square
    sq_far = [
        send(
            "head", far_peer[r], sq_send.at[1], sq_got.at[r], sq_ss.at[r], sq_rs.at[r]
        )
        for r in range(1, chips)
    ]
    for copy in sq_far:
        copy.start()
    kept = []
    for j in range(n_col):
        kept.append(project(0, j))
        if j == 0:
            forward(*held)
    for copy in sq_far:
        copy.wait()
    for r in range(1, chips):
        pair_square = pair_square + sq_got[r]
    total_square = jnp.sum(pair_square, axis=0, keepdims=True)
    norm = lax.rsqrt(total_square / width_all + EPSILON)
    columns = jnp.transpose(jnp.broadcast_to(norm, (LANES, rows)))
    gain_t[pl.ds(0, rows), :] = columns
    me = lax.axis_index("head")
    norm_mine = gain_t[pl.ds(pl.multiple_of(me * block, block), block), :]
    norm_wide = jnp.concatenate([norm_mine] * (col // LANES), axis=1)
    for j in range(n_col):
        core_copy(0, j).wait_recv()
        value = kept[j] + core_got[0, j].astype(F32)
        for r in range(1, chips):
            far_copy(r, j).wait_recv()
            value = value + far_got[r - 1, j].astype(F32)
        out_ref[:, pl.ds(j * col, col)] = (value * norm_wide).astype(BF16)

    for j in range(n_col):
        for r in range(chips):
            core_copy(r, j).wait_send()
        for r in range(1, chips):
            far_copy(r, j).wait_send()
    for g in range(groups):
        for d in range(last):
            state_copy(d, g).wait_send()

        @pl.when(jnp.logical_and(is_source, turn(g)))
        def _():
            cross_copy(g).wait_send()

        @pl.when(jnp.logical_and(is_up, turn(g)))
        def _():
            side_copy(g).wait_send()

        @pl.when(jnp.logical_and(jnp.logical_and(is_up, turn(g)), has_next))
        def _():
            onward_copy(g).wait_send()


def on_device(
    token_values,
    gate_values,
    state_in,
    state_out,
    step_size,
    log_decay,
    level_weight,
    skip_weight,
    norm_gain,
    out_weight,
):
    rows, width = token_values.shape
    heads = step_size.shape[1]
    n_state = state_in.shape[1]
    levels = level_weight.shape[2]
    model = out_weight.shape[1]
    seq_bits = lax.axis_size("seq").bit_length() - 1
    head_devices = lax.axis_size("head")
    group = 4 if heads % 4 == 0 else 2
    groups = heads // group
    span = group * P_SIZE
    chips = head_devices // 2
    col = 512
    n_col = model // col
    block = rows // head_devices
    vmem = pl.BlockSpec(memory_space=pltpu.VMEM)
    hbm = pl.BlockSpec(memory_space=pl.ANY)
    dma = pltpu.SemaphoreType.DMA
    scratch = [
        pltpu.VMEM((rows, width), BF16),
        pltpu.VMEM((rows, width), BF16),
        pltpu.VMEM((rows, n_state), BF16),
        pltpu.VMEM((rows, n_state), BF16),
        pltpu.VMEM((heads, rows), F32),
        pltpu.VMEM((heads, rows), F32),
        pltpu.VMEM((levels, heads, rows), BF16),
        pltpu.VMEM((width,), F32),
        pltpu.VMEM((width, model), BF16),
        pltpu.VMEM((width, rows), F32),
        pltpu.VMEM((width, rows), BF16),
        pltpu.VMEM((width, rows), F32),
        pltpu.VMEM((width, rows), F32),
        pltpu.VMEM((width, LANES), F32),
        pltpu.VMEM((rows, width), BF16),
        pltpu.VMEM((levels, heads, rows), F32),
        pltpu.VMEM((heads, rows), F32),
        pltpu.VMEM((rows, heads), F32),
        pltpu.VMEM((heads, rows), F32),
        pltpu.VMEM((rows, rows), F32),
        pltpu.VMEM((LANES, LANES), jnp.int32),
        pltpu.VMEM((seq_bits, groups, span, n_state), BF16),
        pltpu.VMEM((seq_bits, groups, span, n_state), BF16),
        pltpu.VMEM((seq_bits, heads, LANES), F32),
        pltpu.VMEM((seq_bits, heads, LANES), F32),
        pltpu.VMEM((seq_bits, heads, LANES), F32),
        pltpu.VMEM((8, rows), F32),
        pltpu.VMEM((2, 8, rows), F32),
        pltpu.VMEM((chips, 8, rows), F32),
        pltpu.VMEM((chips, n_col, block, col), BF16),
        pltpu.VMEM((chips, n_col, block, col), BF16),
        pltpu.VMEM((chips - 1, n_col, block, col), BF16),
        pltpu.VMEM((chips - 1, n_col, block, col), BF16),
        dma,
        dma((seq_bits, groups)),
        dma((seq_bits, groups)),
        dma((seq_bits,)),
        dma((seq_bits,)),
        dma((chips,)),
        dma((chips,)),
        dma((chips, n_col)),
        dma((chips, n_col)),
        dma((chips - 1, n_col)),
        dma((chips - 1, n_col)),
        dma((8,)),
        dma((groups,)),
    ]
    return pl.pallas_call(
        functools.partial(
            mixer_kernel, seq_bits, float(width * head_devices), col, group, head_devices
        ),
        out_shape=jax.ShapeDtypeStruct((block, model), BF16),
        in_specs=[hbm] * 7 + [pl.BlockSpec(memory_space=pltpu.SMEM), hbm, hbm],
        out_specs=vmem,
        scratch_shapes=scratch,
        compiler_params=pltpu.CompilerParams(
            collective_id=0, has_side_effects=True, vmem_limit_bytes=58 * 1024 * 1024
        ),
        cost_estimate=pl.CostEstimate(
            flops=2 * rows * width * (model + 4 * rows), bytes_accessed=2 * width * model, transcendentals=heads * rows * rows
        ),
        name="mixer",
    )(
        token_values,
        gate_values,
        state_in,
        state_out,
        jnp.transpose(step_size),
        jnp.transpose(log_decay),
        jnp.transpose(level_weight, (2, 1, 0)),
        skip_weight,
        norm_gain,
        out_weight,
    )


def solution(mesh):
    placed = (
        P("seq", "head"),
        P("seq", "head"),
        P("seq", None),
        P("seq", None),
        P("seq", "head"),
        P("seq", "head"),
        P("seq", "head", None),
        P("head"),
        P("head"),
        P("head", None),
    )
    return jax.shard_map(
        on_device, mesh=mesh, in_specs=placed, out_specs=P(("seq", "head"), None), check_vma=False
    )
```

```python
import functools

import jax
import jax.numpy as jnp
from jax import lax
from jax.experimental import pallas as pl
from jax.experimental.pallas import tpu as pltpu
from jax.sharding import PartitionSpec as P

P_SIZE = 64
EPSILON = 1e-05
HIGH = lax.Precision.HIGHEST
MESH = pl.DeviceIdType.MESH
LANES = 128
F32 = jnp.float32
BF16 = jnp.bfloat16


def dot(a, b, precision=None):
    return jnp.dot(a, b, preferred_element_type=F32, precision=precision)


def dot_nt(a, b):
    return lax.dot_general(a, b, (((1,), (1,)), ((), ())), preferred_element_type=F32)


def partner_of(axis, depth):
    me = lax.axis_index(axis)
    bit = (me // 2**depth) % 2
    return bit, me + (1 - 2 * bit) * 2**depth


def mixer_kernel(
    seq_bits,
    width_all,
    col,
    GROUP,
    head_devices,
    tv_hbm,
    gate_hbm,
    key_hbm,
    query_hbm,
    step_hbm,
    decay_hbm,
    weight_hbm,
    skip_ref,
    gain_hbm,
    w_hbm,
    out_ref,
    tv_ref,
    gate_ref,
    key_ref,
    query_ref,
    step_ref,
    decay_ref,
    weight_ref,
    gain_ref,
    w_ref,
    tvt,
    xt,
    mixed,
    silu_t,
    gain_t,
    feat,
    lw,
    cum_r,
    cum_c,
    lift,
    score_t,
    level_of,
    own,
    got,
    e_own,
    e_got,
    factor,
    square,
    sq_send,
    sq_got,
    core_send,
    core_got,
    far_send,
    far_got,
    w_sem,
    state_ss,
    state_rs,
    e_ss,
    e_rs,
    sq_ss,
    sq_rs,
    core_ss,
    core_rs,
    far_ss,
    far_rs,
    in_sem,
):
    rows = tv_ref.shape[0]
    heads = step_ref.shape[0]
    tiles = rows // LANES
    groups = heads // GROUP
    span = GROUP * P_SIZE
    lane_bits = LANES.bit_length() - 1
    local_bits = rows.bit_length() - 1
    levels_here = local_bits + 1
    n_col = w_ref.shape[1] // col
    block = rows // head_devices
    chips = head_devices // 2

    barrier = pltpu.get_barrier_semaphore()
    seq_partner = [partner_of("seq", d) for d in range(seq_bits)]
    core_bit, core_peer = partner_of("head", 0)
    chip = lax.axis_index("head") // 2
    chip_at = [(chip + r) % chips for r in range(chips)]
    far_peer = [2 * at + core_bit for at in chip_at]
    last = seq_bits - 1
    n_seq = 2**seq_bits
    at_seq = lax.axis_index("seq")
    is_up = at_seq >= n_seq // 2
    for _, peer in seq_partner:
        pl.semaphore_signal(barrier, inc=1, device_id={"seq": peer}, device_id_type=MESH)
    for peer in [core_peer] + far_peer[1:]:
        pl.semaphore_signal(barrier, inc=1, device_id={"head": peer}, device_id_type=MESH)

    pairs = [
        (decay_hbm, decay_ref),
        (step_hbm, step_ref),
        (tv_hbm, tv_ref),
        (key_hbm, key_ref),
        (query_hbm, query_ref),
        (weight_hbm, weight_ref),
        (gate_hbm, gate_ref),
        (gain_hbm, gain_ref),
    ]
    loads = [
        pltpu.make_async_copy(src, dst, in_sem.at[i]) for i, (src, dst) in enumerate(pairs)
    ]
    w_copy = pltpu.make_async_copy(w_hbm, w_ref, w_sem)
    for load in loads:
        load.start()
    w_copy.start()

    def send(axis, peer, src, dst, ss, rs):
        return pltpu.make_async_remote_copy(
            src_ref=src,
            dst_ref=dst,
            send_sem=ss,
            recv_sem=rs,
            device_id={axis: peer},
            device_id_type=MESH,
        )

    def state_copy(d, g):
        return send(
            "seq", seq_partner[d][1], own.at[d, g], got.at[d, g], state_ss.at[d, g], state_rs.at[d, g]
        )

    def total_copy(d):
        return send("seq", seq_partner[d][1], e_own.at[d], e_got.at[d], e_ss.at[d], e_rs.at[d])

    u_at = lax.broadcasted_iota(jnp.int32, (rows, rows), 0)
    t_at = lax.broadcasted_iota(jnp.int32, (rows, rows), 1)
    loads[0].wait()
    decay = decay_ref[...]
    cum = dot(decay, (u_at <= t_at).astype(F32), HIGH)
    to_end = jnp.exp(dot(decay, (u_at > t_at).astype(F32), HIGH))
    total = dot(decay, jnp.ones((rows, LANES), F32), HIGH)
    cum_r[...] = cum
    loads[1].wait()
    steps = step_ref[...]
    key_scale = steps * to_end
    e_own[0] = jnp.exp(total)

    loads[2].wait()
    loads[3].wait()
    pl.semaphore_wait(barrier, seq_bits + chips)
    total_copy(0).start()
    keys = key_ref[...]
    for g in range(groups):
        for j in range(g * span // LANES, (g + 1) * span // LANES):
            tvt[pl.ds(j * LANES, LANES), :] = jnp.transpose(
                tv_ref[:, pl.ds(j * LANES, LANES)].astype(F32)
            )
        parts = []
        for h in range(g * GROUP, (g + 1) * GROUP):
            value = tvt[pl.ds(h * P_SIZE, P_SIZE), :]
            parts.append((value * key_scale[h : h + 1, :]).astype(BF16))
            xt[pl.ds(h * P_SIZE, P_SIZE), :] = (value * steps[h : h + 1, :]).astype(BF16)
        own[0, g] = dot(jnp.concatenate(parts, axis=0), keys).astype(BF16)
        state_copy(0, g).start()

    for load in loads[4:]:
        load.wait()
    lift[...] = jnp.exp(cum)
    cum_c[...] = jnp.transpose(cum)
    for l in range(weight_ref.shape[0]):
        lw[l] = weight_ref[l].astype(F32)
    queries = query_ref[...]
    s_full = dot_nt(keys, queries)
    score_t[...] = jnp.where(u_at <= t_at, s_full, 0.0)
    apart = jnp.bitwise_xor(u_at[:LANES, :LANES], t_at[:LANES, :LANES])
    level = jnp.zeros((LANES, LANES), jnp.int32)
    for shift in range(lane_bits):
        level = level + (apart >= 1 << shift).astype(jnp.int32)
    level_of[...] = level
    square[...] = jnp.zeros_like(square)
    for j in range(gate_ref.shape[1] // LANES):
        gain_t[pl.ds(j * LANES, LANES), :] = jnp.transpose(
            jnp.broadcast_to(gain_ref[pl.ds(j * LANES, LANES)].reshape(1, LANES), (LANES, LANES))
        )

    def local_part(g):
        for h in range(g * GROUP, (g + 1) * GROUP):
            at = pl.ds(h * P_SIZE, P_SIZE)
            x = xt[at, :]
            for bt in range(tiles):
                lanes = pl.ds(bt * LANES, LANES)
                row = cum_r[pl.ds(h, 1), lanes]
                stack = []
                for bs in range(bt + 1):
                    sub = pl.ds(bs * LANES, LANES)
                    column = cum_c[sub, pl.ds(h, 1)]
                    fade = jnp.exp(jnp.minimum(row - column, 0.0)) * score_t[sub, lanes]
                    if bs == bt:
                        level_now = level_of[...]
                        weight = jnp.broadcast_to(lw[0, pl.ds(h, 1), lanes], (LANES, LANES))
                        for l in range(1, lane_bits + 1):
                            weight = jnp.where(level_now == l, lw[l, pl.ds(h, 1), lanes], weight)
                    else:
                        weight = lw[lane_bits + (bt ^ bs).bit_length(), pl.ds(h, 1), lanes]
                    stack.append((fade * weight).astype(BF16))
                mix = stack[0] if bt == 0 else jnp.concatenate(stack, axis=0)
                mixed[at, lanes] = dot(x[:, : (bt + 1) * LANES], mix) + skip_ref[h] * tvt[at, lanes]
        for j in range(g * span // LANES, (g + 1) * span // LANES):
            gate = jnp.transpose(gate_ref[:, pl.ds(j * LANES, LANES)].astype(F32))
            silu_t[pl.ds(j * LANES, LANES), :] = gate / (1.0 + jnp.exp(-gate))

    def add_far(d, g, up):
        reached = dot_nt(got[d, g], query_ref[...])
        for i in range(GROUP):
            h = g * GROUP + i
            at = pl.ds(h * P_SIZE, P_SIZE)
            scale = lw[levels_here + d, pl.ds(h, 1), :] * lift[pl.ds(h, 1), :] * up
            if d > 0:
                reach = factor[d, pl.ds(h, 1), :]
                scale = scale * jnp.concatenate([reach] * tiles, axis=1)
            mixed[at, :] += reached[i * P_SIZE : (i + 1) * P_SIZE] * scale

    def far_part(d, g):
        bit, _ = seq_partner[d]
        up = bit.astype(F32)
        if g == 0:
            total_copy(d).wait()
            mine, theirs = e_own[d], e_got[d]
            reach = jnp.ones_like(mine) if d == 0 else factor[d]
            factor[d + 1] = reach * (up * theirs + (1.0 - up))
            if d + 1 < last:
                e_own[d + 1] = mine * theirs
                total_copy(d + 1).start()
        state_copy(d, g).wait_recv()
        mine, theirs = e_own[d], e_got[d]
        keep = up + (1.0 - up) * theirs
        take = up * mine + (1.0 - up)
        for i in range(GROUP):
            h = g * GROUP + i
            at = pl.ds(i * P_SIZE, P_SIZE)
            own[d + 1, g, at, :] = (
                own[d, g, at, :].astype(F32) * keep[h : h + 1, :]
                + got[d, g, at, :].astype(F32) * take[h : h + 1, :]
            ).astype(BF16)
        if d + 1 < last:
            state_copy(d + 1, g).start()
        else:

            @pl.when(at_seq < n_seq // 2)
            def _():
                state_copy(last, g).start()

        add_far(d, g, up)

    def last_part(g):
        @pl.when(is_up)
        def _():
            state_copy(last, g).wait_recv()
            add_far(last, g, 1.0)

    def finish_group(g):
        at = pl.ds(g * span, span)
        gated = mixed[at, :] * silu_t[at, :]
        square[...] += jnp.sum((gated * gated).reshape(span // 8, 8, rows), axis=0)
        gain = jnp.concatenate([gain_t[at, :]] * tiles, axis=1)
        feat[:, at] = jnp.transpose(gated * gain).astype(BF16)

    for k in range(groups + seq_bits):
        if k < groups:
            local_part(k)
        for d in range(seq_bits):
            g = k - d
            if 0 <= g < groups:
                if d < last:
                    far_part(d, g)
                else:
                    last_part(g)
                    finish_group(g)

    sq_send[0] = square[...]
    sq_core = send("head", core_peer, sq_send.at[0], sq_got.at[0], sq_ss.at[0], sq_rs.at[0])
    sq_core.start()
    w_copy.wait()

    def core_copy(part, j):
        return send(
            "head",
            core_peer,
            core_send.at[part, j],
            core_got.at[part, j],
            core_ss.at[part, j],
            core_rs.at[part, j],
        )

    def far_copy(r, j):
        return send(
            "head",
            far_peer[r],
            far_send.at[r - 1, j],
            far_got.at[r - 1, j],
            far_ss.at[r - 1, j],
            far_rs.at[r - 1, j],
        )

    mine_at = core_bit * block
    theirs_at = (1 - core_bit) * block

    def project(r, j):
        wide = pl.ds(j * col, col)
        at = chip_at[r] * (2 * block)
        theirs = feat[pl.ds(pl.multiple_of(at + theirs_at, block), block), :]
        mine = feat[pl.ds(pl.multiple_of(at + mine_at, block), block), :]
        product = dot(jnp.concatenate([theirs, mine], axis=0), w_ref[:, wide])
        core_send[r, j] = product[:block].astype(BF16)
        core_copy(r, j).start()
        return product[block:]

    def forward(r, j, value):
        core_copy(r, j).wait_recv()
        far_send[r - 1, j] = (value + core_got[r, j].astype(F32)).astype(BF16)
        far_copy(r, j).start()

    held = None
    for r in range(1, chips):
        for j in range(n_col):
            fresh = project(r, j)
            if held is not None:
                forward(*held)
            held = (r, j, fresh)
    sq_core.wait()
    pair_square = square[...] + sq_got[0]
    sq_send[1] = pair_square
    sq_far = [
        send(
            "head", far_peer[r], sq_send.at[1], sq_got.at[r], sq_ss.at[r], sq_rs.at[r]
        )
        for r in range(1, chips)
    ]
    for copy in sq_far:
        copy.start()
    kept = []
    for j in range(n_col):
        kept.append(project(0, j))
        if j == 0:
            forward(*held)
    for copy in sq_far:
        copy.wait()
    for r in range(1, chips):
        pair_square = pair_square + sq_got[r]
    total_square = jnp.sum(pair_square, axis=0, keepdims=True)
    norm = lax.rsqrt(total_square / width_all + EPSILON)
    columns = jnp.transpose(jnp.broadcast_to(norm, (LANES, rows)))
    gain_t[pl.ds(0, rows), :] = columns
    me = lax.axis_index("head")
    norm_mine = gain_t[pl.ds(pl.multiple_of(me * block, block), block), :]
    norm_wide = jnp.concatenate([norm_mine] * (col // LANES), axis=1)
    for j in range(n_col):
        core_copy(0, j).wait_recv()
        value = kept[j] + core_got[0, j].astype(F32)
        for r in range(1, chips):
            far_copy(r, j).wait_recv()
            value = value + far_got[r - 1, j].astype(F32)
        out_ref[:, pl.ds(j * col, col)] = (value * norm_wide).astype(BF16)

    for j in range(n_col):
        for r in range(chips):
            core_copy(r, j).wait_send()
        for r in range(1, chips):
            far_copy(r, j).wait_send()
    for g in range(groups):
        for d in range(last):
            state_copy(d, g).wait_send()

        @pl.when(at_seq < n_seq // 2)
        def _():
            state_copy(last, g).wait_send()


def on_device(
    token_values,
    gate_values,
    state_in,
    state_out,
    step_size,
    log_decay,
    level_weight,
    skip_weight,
    norm_gain,
    out_weight,
):
    rows, width = token_values.shape
    heads = step_size.shape[1]
    n_state = state_in.shape[1]
    levels = level_weight.shape[2]
    model = out_weight.shape[1]
    seq_bits = lax.axis_size("seq").bit_length() - 1
    head_devices = lax.axis_size("head")
    group = 4 if heads % 4 == 0 else 2
    groups = heads // group
    span = group * P_SIZE
    chips = head_devices // 2
    col = 512
    n_col = model // col
    block = rows // head_devices
    vmem = pl.BlockSpec(memory_space=pltpu.VMEM)
    hbm = pl.BlockSpec(memory_space=pl.ANY)
    dma = pltpu.SemaphoreType.DMA
    scratch = [
        pltpu.VMEM((rows, width), BF16),
        pltpu.VMEM((rows, width), BF16),
        pltpu.VMEM((rows, n_state), BF16),
        pltpu.VMEM((rows, n_state), BF16),
        pltpu.VMEM((heads, rows), F32),
        pltpu.VMEM((heads, rows), F32),
        pltpu.VMEM((levels, heads, rows), BF16),
        pltpu.VMEM((width,), F32),
        pltpu.VMEM((width, model), BF16),
        pltpu.VMEM((width, rows), F32),
        pltpu.VMEM((width, rows), BF16),
        pltpu.VMEM((width, rows), F32),
        pltpu.VMEM((width, rows), F32),
        pltpu.VMEM((width, LANES), F32),
        pltpu.VMEM((rows, width), BF16),
        pltpu.VMEM((levels, heads, rows), F32),
        pltpu.VMEM((heads, rows), F32),
        pltpu.VMEM((rows, heads), F32),
        pltpu.VMEM((heads, rows), F32),
        pltpu.VMEM((rows, rows), F32),
        pltpu.VMEM((LANES, LANES), jnp.int32),
        pltpu.VMEM((seq_bits, groups, span, n_state), BF16),
        pltpu.VMEM((seq_bits, groups, span, n_state), BF16),
        pltpu.VMEM((seq_bits, heads, LANES), F32),
        pltpu.VMEM((seq_bits, heads, LANES), F32),
        pltpu.VMEM((seq_bits, heads, LANES), F32),
        pltpu.VMEM((8, rows), F32),
        pltpu.VMEM((2, 8, rows), F32),
        pltpu.VMEM((chips, 8, rows), F32),
        pltpu.VMEM((chips, n_col, block, col), BF16),
        pltpu.VMEM((chips, n_col, block, col), BF16),
        pltpu.VMEM((chips - 1, n_col, block, col), BF16),
        pltpu.VMEM((chips - 1, n_col, block, col), BF16),
        dma,
        dma((seq_bits, groups)),
        dma((seq_bits, groups)),
        dma((seq_bits,)),
        dma((seq_bits,)),
        dma((chips,)),
        dma((chips,)),
        dma((chips, n_col)),
        dma((chips, n_col)),
        dma((chips - 1, n_col)),
        dma((chips - 1, n_col)),
        dma((8,)),
    ]
    return pl.pallas_call(
        functools.partial(
            mixer_kernel, seq_bits, float(width * head_devices), col, group, head_devices
        ),
        out_shape=jax.ShapeDtypeStruct((block, model), BF16),
        in_specs=[hbm] * 7 + [pl.BlockSpec(memory_space=pltpu.SMEM), hbm, hbm],
        out_specs=vmem,
        scratch_shapes=scratch,
        compiler_params=pltpu.CompilerParams(
            collective_id=0, has_side_effects=True, vmem_limit_bytes=58 * 1024 * 1024
        ),
        cost_estimate=pl.CostEstimate(
            flops=2 * rows * width * (model + 4 * rows), bytes_accessed=2 * width * model, transcendentals=heads * rows * rows
        ),
        name="mixer",
    )(
        token_values,
        gate_values,
        state_in,
        state_out,
        jnp.transpose(step_size),
        jnp.transpose(log_decay),
        jnp.transpose(level_weight, (2, 1, 0)),
        skip_weight,
        norm_gain,
        out_weight,
    )


def solution(mesh):
    placed = (
        P("seq", "head"),
        P("seq", "head"),
        P("seq", None),
        P("seq", None),
        P("seq", "head"),
        P("seq", "head"),
        P("seq", "head", None),
        P("head"),
        P("head"),
        P("head", None),
    )
    return jax.shard_map(
        on_device, mesh=mesh, in_specs=placed, out_specs=P(("seq", "head"), None), check_vma=False
    )
```

```python
import functools

import jax
import jax.numpy as jnp
from jax import lax
from jax.experimental import pallas as pl
from jax.experimental.pallas import tpu as pltpu
from jax.sharding import PartitionSpec as P

P_SIZE = 64
EPSILON = 1e-05
HIGH = lax.Precision.HIGHEST
MESH = pl.DeviceIdType.MESH
LANES = 128
F32 = jnp.float32
BF16 = jnp.bfloat16


def dot(a, b, precision=None):
    return jnp.dot(a, b, preferred_element_type=F32, precision=precision)


def dot_nt(a, b):
    return lax.dot_general(a, b, (((1,), (1,)), ((), ())), preferred_element_type=F32)


def partner_of(axis, depth):
    me = lax.axis_index(axis)
    bit = (me // 2**depth) % 2
    return bit, me + (1 - 2 * bit) * 2**depth


def mixer_kernel(
    seq_bits,
    width_all,
    col,
    GROUP,
    head_devices,
    tv_hbm,
    gate_hbm,
    key_hbm,
    query_hbm,
    step_hbm,
    decay_hbm,
    weight_hbm,
    skip_ref,
    gain_hbm,
    w_hbm,
    out_ref,
    tv_ref,
    gate_ref,
    key_ref,
    query_ref,
    step_ref,
    decay_ref,
    weight_ref,
    gain_ref,
    w_ref,
    tvt,
    xt,
    mixed,
    silu_t,
    gain_t,
    feat,
    lw,
    cum_r,
    cum_c,
    lift,
    score_t,
    level_of,
    own,
    got,
    e_own,
    e_got,
    factor,
    square,
    sq_send,
    sq_got,
    core_send,
    core_got,
    far_send,
    far_got,
    w_sem,
    state_ss,
    state_rs,
    e_ss,
    e_rs,
    sq_ss,
    sq_rs,
    core_ss,
    core_rs,
    far_ss,
    far_rs,
    in_sem,
):
    rows = tv_ref.shape[0]
    heads = step_ref.shape[0]
    tiles = rows // LANES
    groups = heads // GROUP
    span = GROUP * P_SIZE
    lane_bits = LANES.bit_length() - 1
    local_bits = rows.bit_length() - 1
    levels_here = local_bits + 1
    n_col = w_ref.shape[1] // col
    block = rows // head_devices
    chips = head_devices // 2

    barrier = pltpu.get_barrier_semaphore()
    seq_partner = [partner_of("seq", d) for d in range(seq_bits)]
    core_bit, core_peer = partner_of("head", 0)
    chip = lax.axis_index("head") // 2
    chip_at = [(chip + r) % chips for r in range(chips)]
    far_peer = [2 * at + core_bit for at in chip_at]
    last = seq_bits - 1
    n_seq = 2**seq_bits
    at_seq = lax.axis_index("seq")
    is_up = at_seq >= n_seq // 2
    for _, peer in seq_partner:
        pl.semaphore_signal(barrier, inc=1, device_id={"seq": peer}, device_id_type=MESH)
    for peer in [core_peer] + far_peer[1:]:
        pl.semaphore_signal(barrier, inc=1, device_id={"head": peer}, device_id_type=MESH)

    pairs = [
        (decay_hbm, decay_ref),
        (step_hbm, step_ref),
        (tv_hbm, tv_ref),
        (key_hbm, key_ref),
        (query_hbm, query_ref),
        (weight_hbm, weight_ref),
        (gate_hbm, gate_ref),
        (gain_hbm, gain_ref),
    ]
    loads = [
        pltpu.make_async_copy(src, dst, in_sem.at[i]) for i, (src, dst) in enumerate(pairs)
    ]
    w_copy = pltpu.make_async_copy(w_hbm, w_ref, w_sem)
    for load in loads:
        load.start()
    w_copy.start()

    def send(axis, peer, src, dst, ss, rs):
        return pltpu.make_async_remote_copy(
            src_ref=src,
            dst_ref=dst,
            send_sem=ss,
            recv_sem=rs,
            device_id={axis: peer},
            device_id_type=MESH,
        )

    def state_copy(d, g):
        return send(
            "seq", seq_partner[d][1], own.at[d, g], got.at[d, g], state_ss.at[d, g], state_rs.at[d, g]
        )

    def total_copy(d):
        return send("seq", seq_partner[d][1], e_own.at[d], e_got.at[d], e_ss.at[d], e_rs.at[d])

    u_at = lax.broadcasted_iota(jnp.int32, (rows, rows), 0)
    t_at = lax.broadcasted_iota(jnp.int32, (rows, rows), 1)
    loads[0].wait()
    decay = decay_ref[...]
    cum = dot(decay, (u_at <= t_at).astype(F32), HIGH)
    to_end = jnp.exp(dot(decay, (u_at > t_at).astype(F32), HIGH))
    total = dot(decay, jnp.ones((rows, LANES), F32), HIGH)
    cum_r[...] = cum
    loads[1].wait()
    steps = step_ref[...]
    key_scale = steps * to_end
    e_own[0] = jnp.exp(total)

    loads[2].wait()
    loads[3].wait()
    pl.semaphore_wait(barrier, seq_bits + chips)
    total_copy(0).start()
    keys = key_ref[...]
    for g in range(groups):
        for j in range(g * span // LANES, (g + 1) * span // LANES):
            tvt[pl.ds(j * LANES, LANES), :] = jnp.transpose(
                tv_ref[:, pl.ds(j * LANES, LANES)].astype(F32)
            )
        parts = []
        for h in range(g * GROUP, (g + 1) * GROUP):
            value = tvt[pl.ds(h * P_SIZE, P_SIZE), :]
            parts.append((value * key_scale[h : h + 1, :]).astype(BF16))
            xt[pl.ds(h * P_SIZE, P_SIZE), :] = (value * steps[h : h + 1, :]).astype(BF16)
        own[0, g] = dot(jnp.concatenate(parts, axis=0), keys).astype(BF16)
        state_copy(0, g).start()

    for load in loads[4:]:
        load.wait()
    lift[...] = jnp.exp(cum)
    cum_c[...] = jnp.transpose(cum)
    for l in range(weight_ref.shape[0]):
        lw[l] = weight_ref[l].astype(F32)
    queries = query_ref[...]
    s_full = dot_nt(keys, queries)
    score_t[...] = jnp.where(u_at <= t_at, s_full, 0.0)
    apart = jnp.bitwise_xor(u_at[:LANES, :LANES], t_at[:LANES, :LANES])
    level = jnp.zeros((LANES, LANES), jnp.int32)
    for shift in range(lane_bits):
        level = level + (apart >= 1 << shift).astype(jnp.int32)
    level_of[...] = level.astype(BF16)
    square[...] = jnp.zeros_like(square)
    for j in range(gate_ref.shape[1] // LANES):
        gain_t[pl.ds(j * LANES, LANES), :] = jnp.transpose(
            jnp.broadcast_to(gain_ref[pl.ds(j * LANES, LANES)].reshape(1, LANES), (LANES, LANES))
        )

    def local_part(g):
        for h in range(g * GROUP, (g + 1) * GROUP):
            at = pl.ds(h * P_SIZE, P_SIZE)
            x = xt[at, :]
            for bt in range(tiles):
                lanes = pl.ds(bt * LANES, LANES)
                row = cum_r[pl.ds(h, 1), lanes]
                stack = []
                for bs in range(bt + 1):
                    sub = pl.ds(bs * LANES, LANES)
                    column = cum_c[sub, pl.ds(h, 1)]
                    fade = jnp.exp(jnp.minimum(row - column, 0.0)) * score_t[sub, lanes]
                    if bs == bt:
                        level_now = level_of[...]
                        narrow = [
                            jnp.broadcast_to(lw[l, pl.ds(h, 1), lanes].astype(BF16), (LANES, LANES))
                            for l in range(lane_bits + 1)
                        ]
                        weight = narrow[0]
                        for l in range(1, lane_bits + 1):
                            weight = jnp.where(level_now == l, narrow[l], weight)
                        stack.append(fade.astype(BF16) * weight)
                    else:
                        weight = lw[lane_bits + (bt ^ bs).bit_length(), pl.ds(h, 1), lanes]
                        stack.append((fade * weight).astype(BF16))
                mix = stack[0] if bt == 0 else jnp.concatenate(stack, axis=0)
                mixed[at, lanes] = dot(x[:, : (bt + 1) * LANES], mix) + skip_ref[h] * tvt[at, lanes]
        for j in range(g * span // LANES, (g + 1) * span // LANES):
            gate = jnp.transpose(gate_ref[:, pl.ds(j * LANES, LANES)].astype(F32))
            silu_t[pl.ds(j * LANES, LANES), :] = gate / (1.0 + jnp.exp(-gate))

    def add_far(d, g, up):
        reached = dot_nt(got[d, g], query_ref[...])
        for i in range(GROUP):
            h = g * GROUP + i
            at = pl.ds(h * P_SIZE, P_SIZE)
            scale = lw[levels_here + d, pl.ds(h, 1), :] * lift[pl.ds(h, 1), :] * up
            if d > 0:
                reach = factor[d, pl.ds(h, 1), :]
                scale = scale * jnp.concatenate([reach] * tiles, axis=1)
            mixed[at, :] += reached[i * P_SIZE : (i + 1) * P_SIZE] * scale

    def far_part(d, g):
        bit, _ = seq_partner[d]
        up = bit.astype(F32)
        if g == 0:
            total_copy(d).wait()
            mine, theirs = e_own[d], e_got[d]
            reach = jnp.ones_like(mine) if d == 0 else factor[d]
            factor[d + 1] = reach * (up * theirs + (1.0 - up))
            if d + 1 < last:
                e_own[d + 1] = mine * theirs
                total_copy(d + 1).start()
        state_copy(d, g).wait_recv()
        mine, theirs = e_own[d], e_got[d]
        keep = up + (1.0 - up) * theirs
        take = up * mine + (1.0 - up)
        for i in range(GROUP):
            h = g * GROUP + i
            at = pl.ds(i * P_SIZE, P_SIZE)
            own[d + 1, g, at, :] = (
                own[d, g, at, :].astype(F32) * keep[h : h + 1, :]
                + got[d, g, at, :].astype(F32) * take[h : h + 1, :]
            ).astype(BF16)
        if d + 1 < last:
            state_copy(d + 1, g).start()
        else:

            @pl.when(at_seq < n_seq // 2)
            def _():
                state_copy(last, g).start()

        add_far(d, g, up)

    def last_part(g):
        @pl.when(is_up)
        def _():
            state_copy(last, g).wait_recv()
            add_far(last, g, 1.0)

    def finish_group(g):
        at = pl.ds(g * span, span)
        gated = mixed[at, :] * silu_t[at, :]
        square[...] += jnp.sum((gated * gated).reshape(span // 8, 8, rows), axis=0)
        gain = jnp.concatenate([gain_t[at, :]] * tiles, axis=1)
        feat[:, at] = jnp.transpose(gated * gain).astype(BF16)

    for k in range(groups + seq_bits):
        if k < groups:
            local_part(k)
        for d in range(seq_bits):
            g = k - d
            if 0 <= g < groups:
                if d < last:
                    far_part(d, g)
                else:
                    last_part(g)
                    finish_group(g)

    sq_send[0] = square[...]
    sq_core = send("head", core_peer, sq_send.at[0], sq_got.at[0], sq_ss.at[0], sq_rs.at[0])
    sq_core.start()
    w_copy.wait()

    def core_copy(part, j):
        return send(
            "head",
            core_peer,
            core_send.at[part, j],
            core_got.at[part, j],
            core_ss.at[part, j],
            core_rs.at[part, j],
        )

    def far_copy(r, j):
        return send(
            "head",
            far_peer[r],
            far_send.at[r - 1, j],
            far_got.at[r - 1, j],
            far_ss.at[r - 1, j],
            far_rs.at[r - 1, j],
        )

    mine_at = core_bit * block
    theirs_at = (1 - core_bit) * block

    def project(r, j):
        wide = pl.ds(j * col, col)
        at = chip_at[r] * (2 * block)
        theirs = feat[pl.ds(pl.multiple_of(at + theirs_at, block), block), :]
        mine = feat[pl.ds(pl.multiple_of(at + mine_at, block), block), :]
        product = dot(jnp.concatenate([theirs, mine], axis=0), w_ref[:, wide])
        core_send[r, j] = product[:block].astype(BF16)
        core_copy(r, j).start()
        return product[block:]

    def forward(r, j, value):
        core_copy(r, j).wait_recv()
        far_send[r - 1, j] = (value + core_got[r, j].astype(F32)).astype(BF16)
        far_copy(r, j).start()

    held = None
    for r in range(1, chips):
        for j in range(n_col):
            fresh = project(r, j)
            if held is not None:
                forward(*held)
            held = (r, j, fresh)
    sq_core.wait()
    pair_square = square[...] + sq_got[0]
    sq_send[1] = pair_square
    sq_far = [
        send(
            "head", far_peer[r], sq_send.at[1], sq_got.at[r], sq_ss.at[r], sq_rs.at[r]
        )
        for r in range(1, chips)
    ]
    for copy in sq_far:
        copy.start()
    kept = []
    for j in range(n_col):
        kept.append(project(0, j))
        if j == 0:
            forward(*held)
    for copy in sq_far:
        copy.wait()
    for r in range(1, chips):
        pair_square = pair_square + sq_got[r]
    total_square = jnp.sum(pair_square, axis=0, keepdims=True)
    norm = lax.rsqrt(total_square / width_all + EPSILON)
    columns = jnp.transpose(jnp.broadcast_to(norm, (LANES, rows)))
    gain_t[pl.ds(0, rows), :] = columns
    me = lax.axis_index("head")
    norm_mine = gain_t[pl.ds(pl.multiple_of(me * block, block), block), :]
    norm_wide = jnp.concatenate([norm_mine] * (col // LANES), axis=1)
    for j in range(n_col):
        core_copy(0, j).wait_recv()
        value = kept[j] + core_got[0, j].astype(F32)
        for r in range(1, chips):
            far_copy(r, j).wait_recv()
            value = value + far_got[r - 1, j].astype(F32)
        out_ref[:, pl.ds(j * col, col)] = (value * norm_wide).astype(BF16)

    for j in range(n_col):
        for r in range(chips):
            core_copy(r, j).wait_send()
        for r in range(1, chips):
            far_copy(r, j).wait_send()
    for g in range(groups):
        for d in range(last):
            state_copy(d, g).wait_send()

        @pl.when(at_seq < n_seq // 2)
        def _():
            state_copy(last, g).wait_send()


def on_device(
    token_values,
    gate_values,
    state_in,
    state_out,
    step_size,
    log_decay,
    level_weight,
    skip_weight,
    norm_gain,
    out_weight,
):
    rows, width = token_values.shape
    heads = step_size.shape[1]
    n_state = state_in.shape[1]
    levels = level_weight.shape[2]
    model = out_weight.shape[1]
    seq_bits = lax.axis_size("seq").bit_length() - 1
    head_devices = lax.axis_size("head")
    group = 4 if heads % 4 == 0 else 2
    groups = heads // group
    span = group * P_SIZE
    chips = head_devices // 2
    col = 512
    n_col = model // col
    block = rows // head_devices
    vmem = pl.BlockSpec(memory_space=pltpu.VMEM)
    hbm = pl.BlockSpec(memory_space=pl.ANY)
    dma = pltpu.SemaphoreType.DMA
    scratch = [
        pltpu.VMEM((rows, width), BF16),
        pltpu.VMEM((rows, width), BF16),
        pltpu.VMEM((rows, n_state), BF16),
        pltpu.VMEM((rows, n_state), BF16),
        pltpu.VMEM((heads, rows), F32),
        pltpu.VMEM((heads, rows), F32),
        pltpu.VMEM((levels, heads, rows), BF16),
        pltpu.VMEM((width,), F32),
        pltpu.VMEM((width, model), BF16),
        pltpu.VMEM((width, rows), F32),
        pltpu.VMEM((width, rows), BF16),
        pltpu.VMEM((width, rows), F32),
        pltpu.VMEM((width, rows), F32),
        pltpu.VMEM((width, LANES), F32),
        pltpu.VMEM((rows, width), BF16),
        pltpu.VMEM((levels, heads, rows), F32),
        pltpu.VMEM((heads, rows), F32),
        pltpu.VMEM((rows, heads), F32),
        pltpu.VMEM((heads, rows), F32),
        pltpu.VMEM((rows, rows), F32),
        pltpu.VMEM((LANES, LANES), BF16),
        pltpu.VMEM((seq_bits, groups, span, n_state), BF16),
        pltpu.VMEM((seq_bits, groups, span, n_state), BF16),
        pltpu.VMEM((seq_bits, heads, LANES), F32),
        pltpu.VMEM((seq_bits, heads, LANES), F32),
        pltpu.VMEM((seq_bits, heads, LANES), F32),
        pltpu.VMEM((8, rows), F32),
        pltpu.VMEM((2, 8, rows), F32),
        pltpu.VMEM((chips, 8, rows), F32),
        pltpu.VMEM((chips, n_col, block, col), BF16),
        pltpu.VMEM((chips, n_col, block, col), BF16),
        pltpu.VMEM((chips - 1, n_col, block, col), BF16),
        pltpu.VMEM((chips - 1, n_col, block, col), BF16),
        dma,
        dma((seq_bits, groups)),
        dma((seq_bits, groups)),
        dma((seq_bits,)),
        dma((seq_bits,)),
        dma((chips,)),
        dma((chips,)),
        dma((chips, n_col)),
        dma((chips, n_col)),
        dma((chips - 1, n_col)),
        dma((chips - 1, n_col)),
        dma((8,)),
    ]
    return pl.pallas_call(
        functools.partial(
            mixer_kernel, seq_bits, float(width * head_devices), col, group, head_devices
        ),
        out_shape=jax.ShapeDtypeStruct((block, model), BF16),
        in_specs=[hbm] * 7 + [pl.BlockSpec(memory_space=pltpu.SMEM), hbm, hbm],
        out_specs=vmem,
        scratch_shapes=scratch,
        compiler_params=pltpu.CompilerParams(
            collective_id=0, has_side_effects=True, vmem_limit_bytes=58 * 1024 * 1024
        ),
        cost_estimate=pl.CostEstimate(
            flops=2 * rows * width * (model + 4 * rows), bytes_accessed=2 * width * model, transcendentals=heads * rows * rows
        ),
        name="mixer",
    )(
        token_values,
        gate_values,
        state_in,
        state_out,
        jnp.transpose(step_size),
        jnp.transpose(log_decay),
        jnp.transpose(level_weight, (2, 1, 0)),
        skip_weight,
        norm_gain,
        out_weight,
    )


def solution(mesh):
    placed = (
        P("seq", "head"),
        P("seq", "head"),
        P("seq", None),
        P("seq", None),
        P("seq", "head"),
        P("seq", "head"),
        P("seq", "head", None),
        P("head"),
        P("head"),
        P("head", None),
    )
    return jax.shard_map(
        on_device, mesh=mesh, in_specs=placed, out_specs=P(("seq", "head"), None), check_vma=False
    )
```

```python
import functools

import jax
import jax.numpy as jnp
from jax import lax
from jax.experimental import pallas as pl
from jax.experimental.pallas import tpu as pltpu
from jax.sharding import PartitionSpec as P

P_SIZE = 64
EPSILON = 1e-05
HIGH = lax.Precision.HIGHEST
MESH = pl.DeviceIdType.MESH
LANES = 128
F32 = jnp.float32
BF16 = jnp.bfloat16


def dot(a, b, precision=None):
    return jnp.dot(a, b, preferred_element_type=F32, precision=precision)


def dot_nt(a, b):
    return lax.dot_general(a, b, (((1,), (1,)), ((), ())), preferred_element_type=F32)


def partner_of(axis, depth):
    me = lax.axis_index(axis)
    bit = (me // 2**depth) % 2
    return bit, me + (1 - 2 * bit) * 2**depth


def mixer_kernel(
    seq_bits,
    width_all,
    col,
    GROUP,
    head_devices,
    tv_hbm,
    gate_hbm,
    key_hbm,
    query_hbm,
    step_hbm,
    decay_hbm,
    weight_hbm,
    skip_ref,
    gain_hbm,
    w_hbm,
    out_ref,
    tv_ref,
    gate_ref,
    key_ref,
    query_ref,
    step_ref,
    decay_ref,
    weight_ref,
    gain_ref,
    w_ref,
    tvt,
    xt,
    mixed,
    silu_t,
    gain_t,
    feat,
    lw,
    cum_r,
    cum_c,
    lift,
    score_t,
    level_of,
    own,
    got,
    e_own,
    e_got,
    factor,
    square,
    sq_send,
    sq_got,
    core_send,
    core_got,
    far_send,
    far_got,
    w_sem,
    state_ss,
    state_rs,
    e_ss,
    e_rs,
    sq_ss,
    sq_rs,
    core_ss,
    core_rs,
    far_ss,
    far_rs,
    in_sem,
):
    rows = tv_ref.shape[0]
    heads = step_ref.shape[0]
    tiles = rows // LANES
    groups = heads // GROUP
    span = GROUP * P_SIZE
    lane_bits = LANES.bit_length() - 1
    local_bits = rows.bit_length() - 1
    levels_here = local_bits + 1
    n_col = w_ref.shape[1] // col
    block = rows // head_devices
    chips = head_devices // 2

    barrier = pltpu.get_barrier_semaphore()
    seq_partner = [partner_of("seq", d) for d in range(seq_bits)]
    core_bit, core_peer = partner_of("head", 0)
    chip = lax.axis_index("head") // 2
    chip_at = [(chip + r) % chips for r in range(chips)]
    far_peer = [2 * at + core_bit for at in chip_at]
    last = seq_bits - 1
    n_seq = 2**seq_bits
    at_seq = lax.axis_index("seq")
    is_up = at_seq >= n_seq // 2
    for _, peer in seq_partner:
        pl.semaphore_signal(barrier, inc=1, device_id={"seq": peer}, device_id_type=MESH)
    for peer in [core_peer] + far_peer[1:]:
        pl.semaphore_signal(barrier, inc=1, device_id={"head": peer}, device_id_type=MESH)

    pairs = [
        (decay_hbm, decay_ref),
        (step_hbm, step_ref),
        (tv_hbm, tv_ref),
        (key_hbm, key_ref),
        (query_hbm, query_ref),
        (weight_hbm, weight_ref),
        (gate_hbm, gate_ref),
        (gain_hbm, gain_ref),
    ]
    loads = [
        pltpu.make_async_copy(src, dst, in_sem.at[i]) for i, (src, dst) in enumerate(pairs)
    ]
    w_copy = pltpu.make_async_copy(w_hbm, w_ref, w_sem)
    for load in loads:
        load.start()
    w_copy.start()

    def send(axis, peer, src, dst, ss, rs):
        return pltpu.make_async_remote_copy(
            src_ref=src,
            dst_ref=dst,
            send_sem=ss,
            recv_sem=rs,
            device_id={axis: peer},
            device_id_type=MESH,
        )

    def state_copy(d, g):
        return send(
            "seq", seq_partner[d][1], own.at[d, g], got.at[d, g], state_ss.at[d, g], state_rs.at[d, g]
        )

    def total_copy(d):
        return send("seq", seq_partner[d][1], e_own.at[d], e_got.at[d], e_ss.at[d], e_rs.at[d])

    u_at = lax.broadcasted_iota(jnp.int32, (rows, rows), 0)
    t_at = lax.broadcasted_iota(jnp.int32, (rows, rows), 1)
    loads[0].wait()
    decay = decay_ref[...]
    cum = dot(decay, (u_at <= t_at).astype(F32), HIGH)
    to_end = jnp.exp(dot(decay, (u_at > t_at).astype(F32), HIGH))
    total = dot(decay, jnp.ones((rows, LANES), F32), HIGH)
    cum_r[...] = cum
    loads[1].wait()
    steps = step_ref[...]
    key_scale = steps * to_end
    e_own[0] = jnp.exp(total)

    loads[2].wait()
    loads[3].wait()
    pl.semaphore_wait(barrier, seq_bits + chips)
    total_copy(0).start()
    keys = key_ref[...]
    for g in range(groups):
        for j in range(g * span // LANES, (g + 1) * span // LANES):
            tvt[pl.ds(j * LANES, LANES), :] = jnp.transpose(
                tv_ref[:, pl.ds(j * LANES, LANES)].astype(F32)
            )
        parts = []
        for h in range(g * GROUP, (g + 1) * GROUP):
            value = tvt[pl.ds(h * P_SIZE, P_SIZE), :]
            parts.append((value * key_scale[h : h + 1, :]).astype(BF16))
            xt[pl.ds(h * P_SIZE, P_SIZE), :] = (value * steps[h : h + 1, :]).astype(BF16)
        own[0, g] = dot(jnp.concatenate(parts, axis=0), keys).astype(BF16)
        state_copy(0, g).start()

    for load in loads[4:]:
        load.wait()
    lift[...] = jnp.exp(cum)
    cum_c[...] = jnp.transpose(cum)
    for l in range(weight_ref.shape[0]):
        lw[l] = weight_ref[l].astype(F32)
    queries = query_ref[...]
    s_full = dot_nt(keys, queries)
    score_t[...] = jnp.where(u_at <= t_at, s_full, 0.0)
    apart = jnp.bitwise_xor(u_at[:LANES, :LANES], t_at[:LANES, :LANES])
    level = jnp.zeros((LANES, LANES), jnp.int32)
    for shift in range(lane_bits):
        level = level + (apart >= 1 << shift).astype(jnp.int32)
    level_of[...] = level
    square[...] = jnp.zeros_like(square)
    for j in range(gate_ref.shape[1] // LANES):
        gain_t[pl.ds(j * LANES, LANES), :] = jnp.transpose(
            jnp.broadcast_to(gain_ref[pl.ds(j * LANES, LANES)].reshape(1, LANES), (LANES, LANES))
        )

    def local_part(g):
        for h in range(g * GROUP, (g + 1) * GROUP):
            at = pl.ds(h * P_SIZE, P_SIZE)
            x = xt[at, :]
            for bt in range(tiles):
                lanes = pl.ds(bt * LANES, LANES)
                row = cum_r[pl.ds(h, 1), lanes]
                stack = []
                for bs in range(bt + 1):
                    sub = pl.ds(bs * LANES, LANES)
                    column = cum_c[sub, pl.ds(h, 1)]
                    fade = jnp.exp(jnp.minimum(row - column, 0.0)) * score_t[sub, lanes]
                    if bs == bt:
                        level_now = level_of[...]
                        weight = jnp.broadcast_to(lw[0, pl.ds(h, 1), lanes], (LANES, LANES))
                        for l in range(1, lane_bits + 1):
                            weight = jnp.where(level_now == l, lw[l, pl.ds(h, 1), lanes], weight)
                    else:
                        weight = lw[lane_bits + (bt ^ bs).bit_length(), pl.ds(h, 1), lanes]
                    stack.append((fade * weight).astype(BF16))
                mix = stack[0] if bt == 0 else jnp.concatenate(stack, axis=0)
                mixed[at, lanes] = dot(x[:, : (bt + 1) * LANES], mix) + skip_ref[h] * tvt[at, lanes]
        for j in range(g * span // LANES, (g + 1) * span // LANES):
            gate = jnp.transpose(gate_ref[:, pl.ds(j * LANES, LANES)].astype(F32))
            silu_t[pl.ds(j * LANES, LANES), :] = gate / (1.0 + jnp.exp(-gate))

    def add_far(d, g, up):
        reached = dot_nt(got[d, g], query_ref[...])
        for i in range(GROUP):
            h = g * GROUP + i
            at = pl.ds(h * P_SIZE, P_SIZE)
            scale = lw[levels_here + d, pl.ds(h, 1), :] * lift[pl.ds(h, 1), :] * up
            if d > 0:
                reach = factor[d, pl.ds(h, 1), :]
                scale = scale * jnp.concatenate([reach] * tiles, axis=1)
            mixed[at, :] += reached[i * P_SIZE : (i + 1) * P_SIZE] * scale

    def far_part(d, g):
        bit, _ = seq_partner[d]
        up = bit.astype(F32)
        if g == 0:
            total_copy(d).wait()
            mine, theirs = e_own[d], e_got[d]
            reach = jnp.ones_like(mine) if d == 0 else factor[d]
            factor[d + 1] = reach * (up * theirs + (1.0 - up))
            if d + 1 < last:
                e_own[d + 1] = mine * theirs
                total_copy(d + 1).start()
        state_copy(d, g).wait_recv()
        mine, theirs = e_own[d], e_got[d]
        keep = up + (1.0 - up) * theirs
        take = up * mine + (1.0 - up)
        for i in range(GROUP):
            h = g * GROUP + i
            at = pl.ds(i * P_SIZE, P_SIZE)
            own[d + 1, g, at, :] = (
                own[d, g, at, :].astype(F32) * keep[h : h + 1, :]
                + got[d, g, at, :].astype(F32) * take[h : h + 1, :]
            ).astype(BF16)
        if d + 1 < last:
            state_copy(d + 1, g).start()
        else:

            @pl.when(at_seq < n_seq // 2)
            def _():
                state_copy(last, g).start()

    def last_part(g):
        @pl.when(is_up)
        def _():
            state_copy(last, g).wait_recv()
            add_far(last, g, 1.0)

    def finish_group(g):
        at = pl.ds(g * span, span)
        gated = mixed[at, :] * silu_t[at, :]
        square[...] += jnp.sum((gated * gated).reshape(span // 8, 8, rows), axis=0)
        gain = jnp.concatenate([gain_t[at, :]] * tiles, axis=1)
        feat[:, at] = jnp.transpose(gated * gain).astype(BF16)

    lag = max(3, last + 1)
    for k in range(groups + lag):
        if k < groups:
            local_part(k)
        for d in range(last):
            for g in (2 * (k - d), 2 * (k - d) + 1):
                if 0 <= g < groups:
                    far_part(d, g)
        if k >= lag:
            g = k - lag
            for d in range(last):
                add_far(d, g, seq_partner[d][0].astype(F32))
            last_part(g)
            finish_group(g)

    sq_send[0] = square[...]
    sq_core = send("head", core_peer, sq_send.at[0], sq_got.at[0], sq_ss.at[0], sq_rs.at[0])
    sq_core.start()
    w_copy.wait()

    def core_copy(part, j):
        return send(
            "head",
            core_peer,
            core_send.at[part, j],
            core_got.at[part, j],
            core_ss.at[part, j],
            core_rs.at[part, j],
        )

    def far_copy(r, j):
        return send(
            "head",
            far_peer[r],
            far_send.at[r - 1, j],
            far_got.at[r - 1, j],
            far_ss.at[r - 1, j],
            far_rs.at[r - 1, j],
        )

    mine_at = core_bit * block
    theirs_at = (1 - core_bit) * block

    def project(r, j):
        wide = pl.ds(j * col, col)
        at = chip_at[r] * (2 * block)
        theirs = feat[pl.ds(pl.multiple_of(at + theirs_at, block), block), :]
        mine = feat[pl.ds(pl.multiple_of(at + mine_at, block), block), :]
        product = dot(jnp.concatenate([theirs, mine], axis=0), w_ref[:, wide])
        core_send[r, j] = product[:block].astype(BF16)
        core_copy(r, j).start()
        return product[block:]

    def forward(r, j, value):
        core_copy(r, j).wait_recv()
        far_send[r - 1, j] = (value + core_got[r, j].astype(F32)).astype(BF16)
        far_copy(r, j).start()

    held = None
    for r in range(1, chips):
        for j in range(n_col):
            fresh = project(r, j)
            if held is not None:
                forward(*held)
            held = (r, j, fresh)
    sq_core.wait()
    pair_square = square[...] + sq_got[0]
    sq_send[1] = pair_square
    sq_far = [
        send(
            "head", far_peer[r], sq_send.at[1], sq_got.at[r], sq_ss.at[r], sq_rs.at[r]
        )
        for r in range(1, chips)
    ]
    for copy in sq_far:
        copy.start()
    kept = []
    for j in range(n_col):
        kept.append(project(0, j))
        if j == 0:
            forward(*held)
    for copy in sq_far:
        copy.wait()
    for r in range(1, chips):
        pair_square = pair_square + sq_got[r]
    total_square = jnp.sum(pair_square, axis=0, keepdims=True)
    norm = lax.rsqrt(total_square / width_all + EPSILON)
    columns = jnp.transpose(jnp.broadcast_to(norm, (LANES, rows)))
    gain_t[pl.ds(0, rows), :] = columns
    me = lax.axis_index("head")
    norm_mine = gain_t[pl.ds(pl.multiple_of(me * block, block), block), :]
    norm_wide = jnp.concatenate([norm_mine] * (col // LANES), axis=1)
    for j in range(n_col):
        core_copy(0, j).wait_recv()
        value = kept[j] + core_got[0, j].astype(F32)
        for r in range(1, chips):
            far_copy(r, j).wait_recv()
            value = value + far_got[r - 1, j].astype(F32)
        out_ref[:, pl.ds(j * col, col)] = (value * norm_wide).astype(BF16)

    for j in range(n_col):
        for r in range(chips):
            core_copy(r, j).wait_send()
        for r in range(1, chips):
            far_copy(r, j).wait_send()
    for g in range(groups):
        for d in range(last):
            state_copy(d, g).wait_send()

        @pl.when(at_seq < n_seq // 2)
        def _():
            state_copy(last, g).wait_send()


def on_device(
    token_values,
    gate_values,
    state_in,
    state_out,
    step_size,
    log_decay,
    level_weight,
    skip_weight,
    norm_gain,
    out_weight,
):
    rows, width = token_values.shape
    heads = step_size.shape[1]
    n_state = state_in.shape[1]
    levels = level_weight.shape[2]
    model = out_weight.shape[1]
    seq_bits = lax.axis_size("seq").bit_length() - 1
    head_devices = lax.axis_size("head")
    group = 4 if heads % 4 == 0 else 2
    groups = heads // group
    span = group * P_SIZE
    chips = head_devices // 2
    col = 512
    n_col = model // col
    block = rows // head_devices
    vmem = pl.BlockSpec(memory_space=pltpu.VMEM)
    hbm = pl.BlockSpec(memory_space=pl.ANY)
    dma = pltpu.SemaphoreType.DMA
    scratch = [
        pltpu.VMEM((rows, width), BF16),
        pltpu.VMEM((rows, width), BF16),
        pltpu.VMEM((rows, n_state), BF16),
        pltpu.VMEM((rows, n_state), BF16),
        pltpu.VMEM((heads, rows), F32),
        pltpu.VMEM((heads, rows), F32),
        pltpu.VMEM((levels, heads, rows), BF16),
        pltpu.VMEM((width,), F32),
        pltpu.VMEM((width, model), BF16),
        pltpu.VMEM((width, rows), F32),
        pltpu.VMEM((width, rows), BF16),
        pltpu.VMEM((width, rows), F32),
        pltpu.VMEM((width, rows), F32),
        pltpu.VMEM((width, LANES), F32),
        pltpu.VMEM((rows, width), BF16),
        pltpu.VMEM((levels, heads, rows), F32),
        pltpu.VMEM((heads, rows), F32),
        pltpu.VMEM((rows, heads), F32),
        pltpu.VMEM((heads, rows), F32),
        pltpu.VMEM((rows, rows), F32),
        pltpu.VMEM((LANES, LANES), jnp.int32),
        pltpu.VMEM((seq_bits, groups, span, n_state), BF16),
        pltpu.VMEM((seq_bits, groups, span, n_state), BF16),
        pltpu.VMEM((seq_bits, heads, LANES), F32),
        pltpu.VMEM((seq_bits, heads, LANES), F32),
        pltpu.VMEM((seq_bits, heads, LANES), F32),
        pltpu.VMEM((8, rows), F32),
        pltpu.VMEM((2, 8, rows), F32),
        pltpu.VMEM((chips, 8, rows), F32),
        pltpu.VMEM((chips, n_col, block, col), BF16),
        pltpu.VMEM((chips, n_col, block, col), BF16),
        pltpu.VMEM((chips - 1, n_col, block, col), BF16),
        pltpu.VMEM((chips - 1, n_col, block, col), BF16),
        dma,
        dma((seq_bits, groups)),
        dma((seq_bits, groups)),
        dma((seq_bits,)),
        dma((seq_bits,)),
        dma((chips,)),
        dma((chips,)),
        dma((chips, n_col)),
        dma((chips, n_col)),
        dma((chips - 1, n_col)),
        dma((chips - 1, n_col)),
        dma((8,)),
    ]
    return pl.pallas_call(
        functools.partial(
            mixer_kernel, seq_bits, float(width * head_devices), col, group, head_devices
        ),
        out_shape=jax.ShapeDtypeStruct((block, model), BF16),
        in_specs=[hbm] * 7 + [pl.BlockSpec(memory_space=pltpu.SMEM), hbm, hbm],
        out_specs=vmem,
        scratch_shapes=scratch,
        compiler_params=pltpu.CompilerParams(
            collective_id=0, has_side_effects=True, vmem_limit_bytes=58 * 1024 * 1024
        ),
        cost_estimate=pl.CostEstimate(
            flops=2 * rows * width * (model + 4 * rows), bytes_accessed=2 * width * model, transcendentals=heads * rows * rows
        ),
        name="mixer",
    )(
        token_values,
        gate_values,
        state_in,
        state_out,
        jnp.transpose(step_size),
        jnp.transpose(log_decay),
        jnp.transpose(level_weight, (2, 1, 0)),
        skip_weight,
        norm_gain,
        out_weight,
    )


def solution(mesh):
    placed = (
        P("seq", "head"),
        P("seq", "head"),
        P("seq", None),
        P("seq", None),
        P("seq", "head"),
        P("seq", "head"),
        P("seq", "head", None),
        P("head"),
        P("head"),
        P("head", None),
    )
    return jax.shard_map(
        on_device, mesh=mesh, in_specs=placed, out_specs=P(("seq", "head"), None), check_vma=False
    )
```
